32 devices in a mesh: rx: 4 (over y, x), ry: 8 (over z, core).
Axes of the slice: x: 2, y: 2, z: 4, core: 2. Of those that a mesh axis runs over, the one named last changes fastest.
Arguments:
- propagator: float32 [64, 256, 256], P(('rx', 'ry')), may hold values from -1 to 1, as said below
- forcing: float32 [64, 256, 384], P(('rx', 'ry')), may hold values from -0.9 to 0.9
Outputs:
- solution: float32 [64, 256, 384], P(('rx', 'ry'))
- radial_slope: float32 [64, 256, 384], P(('rx', 'ry'))
The draws below stay inside these ranges and needn't reach their ends.
Inputs may be any that keep to these rules, and one draw needn't show every extreme that they name: Every propagator has spectral norm below 1.
All inputs are finite; a program needn't handle non-finite values.
Results may differ from the reference program's by a relative error of at most 0.00029.
Values sent between devices are 32-bit elements; how exact they have to be, the bound alone decides.
No kernel may reach another device: no remote copies, remote signals or barrier semaphores. Data moves between devices by JAX's collectives and lax.ppermute only.
A program may use at most 64 MiB of HBM per device.

```python
import math
import jax
import jax.numpy as jnp
from jax import lax

B = 256
R = 384
RADIAL_SPANS = 64


def cayley_map(single):
    unit = jnp.eye(single.shape[0], dtype=jnp.float32)
    return jnp.linalg.solve(unit - single, unit + single)


def draw_propagator(key, part):
    asymmetry_key, damping_rate_key, perturbation_key, spike_key = jax.random.split(jax.random.fold_in(key, 17), 4)
    raw = jax.random.normal(asymmetry_key, (RADIAL_SPANS, B, B), jnp.float32) * (0.5 / math.sqrt(B))
    skewed = raw - jnp.transpose(raw, (0, 2, 1))
    rotation = lax.map(cayley_map, skewed)
    low_log = math.log(1.0 / (4.0 * RADIAL_SPANS))
    upper_log = jnp.full((B,), math.log(1.0 / 30.0), jnp.float32)
    fraction = jax.random.uniform(damping_rate_key, (B,), jnp.float32)
    damping_rates = jnp.exp(low_log + fraction * (upper_log - low_log))
    random_perturbation = jax.random.uniform(perturbation_key, (RADIAL_SPANS, B), jnp.float32, 0.5, 1.5)
    spike_locations = jax.random.randint(spike_key, (4,), 0, RADIAL_SPANS)
    positions = jnp.arange(RADIAL_SPANS)
    spike_active = jnp.any(positions[:, None] == spike_locations[None, :], axis=1)
    spike_amplitude = jnp.where(spike_active, 0.6, 1.0).astype(jnp.float32)
    damping_factor = jnp.exp(-damping_rates[None, :] * random_perturbation) * spike_amplitude[:, None]
    return (rotation * damping_factor[:, None, :]).astype(jnp.float32)


def steps_of(own_key, shape, shards, low, largest):
    def one(dim, blocks):
        steps = jax.random.uniform(jax.random.fold_in(jax.random.fold_in(own_key, 6), dim), (blocks,), jnp.float32, low / len(shards), largest / len(shards))
        return jnp.repeat(jnp.exp(steps), shape[dim] // blocks).reshape((-1,) + (1,) * (len(shape) - dim - 1))

    factor_of = one(*shards[0])
    for cut in shards[1:]:
        factor_of = factor_of * one(*cut)
    return factor_of


def centred(own_key, shape, deviation, bound, cuts=(), held_as=jnp.bfloat16):
    loudness = steps_of(own_key, shape, cuts, -0.22, 0.18) if cuts else 1.0
    array = jax.random.normal(own_key, shape, jnp.float32) * deviation * loudness
    return jnp.minimum(jnp.maximum(array, -bound), bound).astype(held_as)


def setup_inputs(seed: int = 0) -> dict:
    seeds = jax.random.split(jax.random.key(seed), 3)
    return {
        "propagator": draw_propagator(jax.random.fold_in(seeds[2], 71), 0),
        "forcing": centred(seeds[1], (RADIAL_SPANS, B, R), 0.15, 0.9, ((0, 32),), jnp.float32),
    }


def reference(propagator, forcing):

    def advance(carried, pieces):
        nextval = jnp.dot(pieces[0].astype(jnp.float32), carried.astype(jnp.float32), precision=lax.Precision.HIGHEST, preferred_element_type=jnp.float32) + pieces[1]
        return (nextval, nextval)
    start = jnp.zeros((B, R), jnp.float32)
    final, solution = lax.scan(advance, start, (propagator, forcing))
    shifted = jnp.concatenate([solution[1:], jnp.zeros((1, B, R), jnp.float32)], axis=0)
    return (solution, shifted - solution)
```

```python
import functools

import jax
import jax.numpy as jnp
from jax import lax
from jax.experimental import pallas as pl
from jax.experimental.pallas import tpu as pltpu
from jax.sharding import PartitionSpec as P

F32 = jnp.float32
NN = (((1,), (0,)), ((), ()))
NT = (((1,), (1,)), ((), ()))


def split(value):
    high = value.astype(jnp.bfloat16)
    return high, (value - high.astype(F32)).astype(jnp.bfloat16)


def product(left, right, dims=NN):
    dot = functools.partial(lax.dot_general, dimension_numbers=dims, preferred_element_type=F32)
    return dot(left[0], right[0]) + (dot(left[0], right[1]) + dot(left[1], right[0]))


def call(kernel, outs, scratch=()):
    spec = pl.BlockSpec(memory_space=pltpu.VMEM)

    def run(*args):
        return pl.pallas_call(
            kernel,
            in_specs=[spec] * len(args),
            out_specs=[spec] * len(outs),
            out_shape=[jax.ShapeDtypeStruct(shape, F32) for shape in outs],
            scratch_shapes=list(scratch),
            compiler_params=pltpu.CompilerParams(vmem_limit_bytes=32 * 1024 * 1024),
        )(*args)

    return run


def local_kernel(a_ref, f_ref, own_ref, first_ref):
    b = a_ref.shape[1]
    first_ref[:, :b] = a_ref[0]
    first_ref[:, b:] = f_ref[0]
    total_a, total_f = a_ref[0], f_ref[0]
    for i in range(1, a_ref.shape[0]):
        step = split(a_ref[i])
        total_a = product(step, split(total_a))
        total_f = product(step, split(total_f)) + f_ref[i]
    own_ref[:, :b] = total_a
    own_ref[:, b:] = total_f


def chip_kernel(heads, own_ref, other_ref, *outs):
    place = lax.axis_index("ry")
    z = place // 2
    b = own_ref.shape[0]
    part = outs[0].shape[0] - b

    @pl.when(place % 2 == 0)
    def _():
        later = split(other_ref[:, :b])
        total_a = product(later, split(own_ref[:, :b])).T
        total_f = (product(later, split(own_ref[:, b:])) + other_ref[:, b:]).T
        for d, out in enumerate(outs):
            for j, head in enumerate(heads):

                @pl.when(z ^ d == head)
                def _():
                    out[:b] = total_a
                    out[b:] = total_f[j * part : (j + 1) * part]


def line_kernel(heads, *refs):
    n = (len(refs) - 3) // 1
    chips = n
    ins, (pre_ref, p_ref, f_ref) = refs[:chips], refs[chips:]
    place = lax.axis_index("ry")
    z = place // 2
    b = p_ref.shape[0]
    is_head = functools.reduce(jnp.logical_or, [z == head for head in heads])

    @pl.when(jnp.logical_and(place % 2 == 0, is_head))
    def _():
        for d in range(chips):
            pre_ref[z ^ d] = ins[d][...]
        total = pre_ref[0]
        for c in range(1, chips):
            here = pre_ref[c]
            pre_ref[c] = total
            step = split(here[:b])
            total = product(split(total), step)
            total = jnp.concatenate([total[:b], total[b:] + here[b:]], axis=0)
        p_ref[...] = total[:b]
        f_ref[...] = total[b:]


def total_kernel(with_map, preP_ref, preF_ref, p_ref, f_ref, outF_ref, *outP):
    step = split(p_ref[...])
    outF_ref[...] = product(split(preF_ref[...]), step) + f_ref[...]
    if with_map:
        outP[0][...] = product(split(preP_ref[...]), step)


def merge(first, state, preP, preF):
    return jnp.where(first, state, product(split(state), split(preP)) + preF)


def prefix_kernel(width, with_map, count, *refs):
    states, maps = refs[:count], refs[count : 2 * count]
    preP_ref, preF_ref, outP_ref, outF_ref = refs[2 * count :]
    g = lax.axis_index("rx")
    upper = (g // width) % 2 == 1
    first = g % (2 * width) == width

    @pl.when(upper)
    def _():
        state = sum(ref[...] for ref in states[1:]) + states[0][...]
        outF_ref[...] = merge(first, state, preP_ref[...], preF_ref[...])
        earlier = sum(ref[...] for ref in maps[1:]) + maps[0][...]
        outP_ref[...] = jnp.where(first, earlier, product(split(earlier), split(preP_ref[...])))

    @pl.when(jnp.logical_not(upper))
    def _():
        outF_ref[...] = preF_ref[...]
        outP_ref[...] = preP_ref[...]


def enter_kernel(width, count, *refs):
    states = refs[:count]
    preP_ref, preF_ref, pre_ref = refs[count : count + 3]
    outs = refs[count + 3 : -1]
    start_ref = refs[-1]
    place = lax.axis_index("ry")
    z = place // 2
    b = preP_ref.shape[0]
    g = lax.axis_index("rx")
    upper = (g // width) % 2 == 1
    first = g % (2 * width) == width
    start_ref[...] = preF_ref[...]
    if count:

        @pl.when(upper)
        def _():
            state = sum(ref[...] for ref in states[1:]) + states[0][...]
            start_ref[...] = merge(first, state, preP_ref[...], preF_ref[...])

    start = split(start_ref[...])
    for c in range(len(outs)):
        state = start_ref[...]
        if c:
            state = product(start, split(pre_ref[c, :b])) + pre_ref[c, b:]
        for d in range(len(outs)):

            @pl.when(z ^ d == c)
            def _():
                outs[d][...] = state


def run_kernel(heads, count, *refs):
    parts, shared = refs[:count], refs[count : 2 * count]
    other_ref, next_ref, a_ref, f_ref, x_ref, s_ref, in_ref, now_ref = refs[2 * count :]
    place = lax.axis_index("ry")
    z = place // 2
    b = a_ref.shape[1]
    part = parts[0].shape[0]
    for core, sources in enumerate((parts, shared)):
        for j, head in enumerate(heads):
            for d in range(count):

                @pl.when(jnp.logical_and(place % 2 == core, z ^ d == head))
                def _():
                    in_ref[j * part : (j + 1) * part] = sources[d][...]

    entering = split(in_ref[...])
    first = split(a_ref[0])

    @pl.when(place % 2 == 0)
    def _():
        now_ref[...] = product(first, entering, NT) + f_ref[0]

    @pl.when(place % 2 == 1)
    def _():
        state = product(split(other_ref[:, :b]), entering, NT) + other_ref[:, b:]
        now_ref[...] = product(first, split(state)) + f_ref[0]

    now = now_ref[...]
    x_ref[0] = now
    for i in range(1, a_ref.shape[0] + 1):
        if i < a_ref.shape[0]:
            later = product(split(a_ref[i]), split(now)) + f_ref[i]
            x_ref[i] = later
        else:
            later = product(split(next_ref[:, :b]), split(now)) + next_ref[:, b:]
        s_ref[i - 1] = later - now
        now = later


def on_device(propagator, forcing):
    intervals, b, r = forcing.shape
    lines, places = lax.axis_size("rx"), lax.axis_size("ry")
    chips = places // 2
    heads = sorted({max(chips // 2 - 1, 0), chips // 2})
    part = r // len(heads)
    both = ("rx", "ry")

    own, first = call(local_kernel, [(b, b + r)] * 2)(propagator, forcing)
    other = lax.ppermute(own, "ry", [(i, i ^ 1) for i in range(places)])
    cuts = call(functools.partial(chip_kernel, heads), [(b + part, b)] * chips)(own, other)
    gathered = [cuts[0]] + [
        lax.ppermute(cuts[d], "ry", [(2 * (h ^ d), 2 * h) for h in heads]) for d in range(1, chips)
    ]
    gathered, first = lax.optimization_barrier((gathered, first))
    following = lax.ppermute(first, both, [(i + 1, i) for i in range(lines * places - 1)])
    prefixes, line_map, line_state = call(
        functools.partial(line_kernel, heads), [(chips, b + part, b), (b, b), (part, b)]
    )(*gathered)

    def hop(value, pairs):
        at = [2 * h for h in heads]
        return lax.ppermute(value, both, [(s * places + i, t * places + i) for s, t in pairs for i in at])

    preP, preF = jnp.zeros((b, b), F32), jnp.zeros((part, b), F32)
    total_map, total_state = line_map, line_state
    width, states = 1, []
    while width < lines:
        starts = range(0, lines, 2 * width)
        with_map = 2 * width < lines
        if width > 1:
            totals = call(functools.partial(total_kernel, with_map), [(part, b)] + [(b, b)] * with_map)(
                preP, preF, line_map, line_state
            )
            total_state, total_map = totals[0], totals[-1]
        sent = [[(s + width - 1, s + width + j) for s in starts] for j in range(width)]
        states = [hop(total_state, pairs) for pairs in sent]
        if not with_map:
            break
        maps = [hop(total_map, [p for p in pairs if p[0] >= width]) for pairs in sent]
        if width == 1:
            preP, preF = maps[0], states[0]
        else:
            preP, preF = call(
                functools.partial(prefix_kernel, width, with_map, len(states)), [(b, b), (part, b)]
            )(*states, *maps, preP, preF)
        width *= 2
    entering = call(
        functools.partial(enter_kernel, width, len(states)),
        [(part, b)] * chips,
        [pltpu.VMEM((part, b), F32)],
    )(*states, preP, preF, prefixes)
    parts = [entering[0]] + [
        lax.ppermute(entering[d], "ry", [(2 * h, 2 * (h ^ d)) for h in heads]) for d in range(1, chips)
    ]
    shared = [lax.ppermute(value, "ry", [(2 * c, 2 * c + 1) for c in range(chips)]) for value in parts]
    return tuple(
        call(
            functools.partial(run_kernel, heads, chips),
            [(intervals, b, r)] * 2,
            [pltpu.VMEM((r, b), F32), pltpu.VMEM((b, r), F32)],
        )(*parts, *shared, other, following, propagator, forcing)
    )


def solution(mesh):
    spec = P(("rx", "ry"), None, None)
    return jax.shard_map(
        on_device, mesh=mesh, in_specs=(spec, spec), out_specs=(spec, spec), check_vma=False
    )
```

```python
import functools

import jax
import jax.numpy as jnp
from jax import lax
from jax.experimental import pallas as pl
from jax.experimental.pallas import tpu as pltpu
from jax.sharding import PartitionSpec as P

F32 = jnp.float32
NN = (((1,), (0,)), ((), ()))
NT = (((1,), (1,)), ((), ()))
VMEM = pl.BlockSpec(memory_space=pltpu.VMEM)
SHADOW = 3_000_000_000
HBM = pl.BlockSpec(memory_space=pltpu.HBM)


def split(value):
    high = value.astype(jnp.bfloat16)
    return high, (value - high.astype(F32)).astype(jnp.bfloat16)


def product(left, right, dims=NN):
    dot = functools.partial(lax.dot_general, dimension_numbers=dims, preferred_element_type=F32)
    return dot(left[0], right[0]) + (dot(left[0], right[1]) + dot(left[1], right[0]))


def call(kernel, outs, scratch=(), spec=VMEM, out_spec=VMEM, flops=None):
    def run(*args):
        return pl.pallas_call(
            kernel,
            in_specs=[spec] * len(args),
            out_specs=[out_spec] * len(outs),
            out_shape=[jax.ShapeDtypeStruct(shape, F32) for shape in outs],
            scratch_shapes=list(scratch),
            cost_estimate=flops and pl.CostEstimate(flops=flops, bytes_accessed=0, transcendentals=0),
            compiler_params=pltpu.CompilerParams(vmem_limit_bytes=32 * 1024 * 1024),
        )(*args)

    return run


def where():
    place = lax.axis_index("ry")
    return lax.axis_index("rx"), place // 2, place % 2


def rows(start, size):
    return pl.ds(pl.multiple_of(start, 8), size)


def local_kernel(a_ref, f_ref, own_ref, first_ref, rest_ref, sems):
    n, b = a_ref.shape[:2]
    copies = []
    for i in range(n):
        to = first_ref if i == 0 else rest_ref.at[i - 1]
        copies.append(
            (
                pltpu.make_async_copy(a_ref.at[i], to.at[:, pl.ds(0, b)], sems.at[i, 0]),
                pltpu.make_async_copy(f_ref.at[i], to.at[:, pl.ds(b, f_ref.shape[2])], sems.at[i, 1]),
            )
        )
    for part in range(2):
        for i in range(n):
            copies[i][part].start()
    copies[0][0].wait()
    total = first_ref[:, :b]
    steps = []
    for i in range(1, n):
        copies[i][0].wait()
        steps.append(split(rest_ref[i - 1, :, :b]))
        total = product(steps[-1], split(total))
    own_ref[:, :b] = total
    copies[0][1].wait()
    total = first_ref[:, b:]
    for i in range(1, n):
        copies[i][1].wait()
        total = product(steps[i - 1], split(total)) + rest_ref[i - 1, :, b:]
    own_ref[:, b:] = total


def chip_kernel(heads, own_ref, other_ref, map_ref, *refs):
    outs, state_ref = refs[:-1], refs[-1]
    _, z, core = where()
    b = own_ref.shape[0]
    part = outs[0].shape[0] - b // 2

    def combine(earlier_ref, later_ref):
        later = split(later_ref[:, :b])
        map_ref[...] = product(later, split(earlier_ref[:, :b])).T
        state_ref[...] = (product(later, split(earlier_ref[:, b:])) + later_ref[:, b:]).T

    @pl.when(core == 0)
    def _():
        combine(own_ref, other_ref)

    @pl.when(core == 1)
    def _():
        combine(other_ref, own_ref)

    for d, out in enumerate(outs):
        for j, head in enumerate(heads):

            @pl.when(z ^ d == head)
            def _():
                out[: b // 2] = map_ref[rows(core * (b // 2), b // 2)]
                out[b // 2 :] = state_ref[rows((2 * j + core) * part, part)]


def line_kernel(heads, chips, *refs):
    map_ref, ins, others = refs[0], refs[1 : 1 + chips], refs[1 + chips : 2 * chips]
    preP_ref, preF_ref, p_ref, f_ref = refs[2 * chips :]
    _, z, core = where()
    b = map_ref.shape[0]
    half = b // 2

    @pl.when(functools.reduce(jnp.logical_or, [z == head for head in heads]))
    def _():
        for d in range(chips):
            preF_ref[z ^ d] = ins[d][half:]
            if d == 0:
                preP_ref[z] = map_ref[...]
            else:
                preP_ref[z ^ d, rows(core * half, half)] = ins[d][:half]
                preP_ref[z ^ d, rows(half - core * half, half)] = others[d - 1][:half]
        total_map, total_state = preP_ref[0], preF_ref[0]
        for c in range(1, chips):
            step, state = split(preP_ref[c]), preF_ref[c]
            preP_ref[c], preF_ref[c] = total_map, total_state
            total_map = product(split(total_map), step)
            total_state = product(split(total_state), step) + state
        p_ref[...] = total_map
        f_ref[...] = total_state


def total_kernel(with_map, *refs):
    *preP, preF_ref, p_ref, f_ref = refs[: 3 + with_map]
    outs = refs[3 + with_map :]
    step = split(p_ref[...])
    outs[0][...] = product(split(preF_ref[...]), step) + f_ref[...]
    if with_map:
        outs[1][...] = product(split(preP[0][...]), step)


def choose(refs, width, out_ref):
    g = where()[0]
    source = g // (2 * width) * (2 * width) + width - 1
    for j, ref in enumerate(refs):

        @pl.when(g ^ (width + j) == source)
        def _():
            out_ref[...] = ref[...]


def prefix_map_kernel(width, *refs):
    *maps, pre_ref, out_ref = refs
    g = where()[0]

    @pl.when(g // width % 2 == 0)
    def _():
        out_ref[...] = pre_ref[...]

    @pl.when(g // width % 2 == 1)
    def _():
        choose(maps, width, out_ref)

        @pl.when(g % width != 0)
        def _():
            out_ref[...] = product(split(out_ref[...]), split(pre_ref[...]))


def advance(width, states, pre, out_ref):
    g = where()[0]

    @pl.when(g // width % 2 == 1)
    def _():
        choose(states, width, out_ref)
        if pre:

            @pl.when(g % width != 0)
            def _():
                out_ref[...] = product(split(out_ref[...]), split(pre[0][...])) + pre[1][...]

    if pre:

        @pl.when(g // width % 2 == 0)
        def _():
            out_ref[...] = pre[1][...]


def prefix_state_kernel(width, count, *refs):
    advance(width, refs[:count], refs[count:-1], refs[-1])


def enter_kernel(width, count, with_pre, *refs):
    states, refs = refs[:count], refs[count:]
    pre, refs = refs[: 2 * with_pre], refs[2 * with_pre :]
    lineP_ref, lineF_ref, *outs, start_ref = refs
    g, z, _ = where()
    if count:
        advance(width, states, pre, start_ref)

    @pl.when(g == 0)
    def _():
        start_ref[...] = jnp.zeros_like(start_ref)

    start = split(start_ref[...])
    for c in range(len(outs)):
        state = start_ref[...]
        if c:
            state = product(start, split(lineP_ref[c])) + lineF_ref[c]
        for d in range(len(outs)):

            @pl.when(z ^ d == c)
            def _():
                outs[d][...] = state


def run_kernel(heads, count, *refs):
    parts, shared = refs[:count], refs[count : 2 * count]
    other_ref, next_ref, first_ref, rest_ref, x_ref, s_ref, in_ref, xs_ref, ss_ref, sems = refs[2 * count :]
    g, z, core = where()
    b = first_ref.shape[0]
    n = x_ref.shape[0]
    part = parts[0].shape[0]
    for d in range(count):
        for j, head in enumerate(heads):

            @pl.when(z ^ d == head)
            def _():
                in_ref[rows((2 * j + core) * part, part)] = parts[d][...]
                in_ref[rows((2 * j + 1 - core) * part, part)] = shared[d][...]

    entering = split(in_ref[...])
    step = split(first_ref[:, :b])

    @pl.when(core == 0)
    def _():
        xs_ref[0] = product(step, entering, NT) + first_ref[:, b:]

    @pl.when(core == 1)
    def _():
        state = product(split(other_ref[:, :b]), entering, NT) + other_ref[:, b:]
        xs_ref[0] = product(step, split(state)) + first_ref[:, b:]

    copies = [pltpu.make_async_copy(xs_ref.at[i], x_ref.at[i], sems.at[0, i]) for i in range(n)]
    copies += [pltpu.make_async_copy(ss_ref.at[i], s_ref.at[i], sems.at[1, i]) for i in range(n)]
    copies[0].start()
    now = xs_ref[0]
    for i in range(1, n):
        later = product(split(rest_ref[i - 1, :, :b]), split(now)) + rest_ref[i - 1, :, b:]
        xs_ref[i] = later
        copies[i].start()
        ss_ref[i - 1] = later - now
        copies[n + i - 1].start()
        now = later
    ss_ref[n - 1] = product(split(next_ref[:, :b]), split(now)) + next_ref[:, b:] - now

    @pl.when(g * lax.axis_size("ry") + 2 * z + core == lax.axis_size("rx") * lax.axis_size("ry") - 1)
    def _():
        ss_ref[n - 1] = -xs_ref[n - 1]

    copies[2 * n - 1].start()
    for copy in copies:
        copy.wait()


def filled(useful, chips):
    sources = [c for c in range(chips) if all(c != s for s, _ in useful)]
    targets = [c for c in range(chips) if all(c != t for _, t in useful)]
    pairs = []
    for s, t in [*useful, *zip(sources, targets, strict=True)]:
        pairs += [(2 * s + core, 2 * t + (core ^ (s == t))) for core in range(2)]
    return pairs


def on_device(propagator, forcing):
    intervals, b, r = forcing.shape
    lines, places = lax.axis_size("rx"), lax.axis_size("ry")
    chips, devices = places // 2, lines * places
    heads = sorted({max(chips // 2 - 1, 0), chips // 2})
    part = r // (2 * len(heads))

    def swap(value):
        return lax.ppermute(value, "ry", [(i, i ^ 1) for i in range(places)])

    def hop(value, d, start=0):
        pairs = []
        for g in range(lines):
            for i in range(places):
                at, to = (g ^ d, i) if i // 2 in heads and g >= start else (g, i ^ 1)
                pairs.append((g * places + i, at * places + to))
        return lax.ppermute(value, ("rx", "ry"), pairs)

    propagator, forcing = (pltpu.with_memory_space_constraint(a, pltpu.HBM) for a in (propagator, forcing))
    own, first, rest = call(
        local_kernel,
        [(b, b + r), (b, b + r), (max(intervals - 1, 1), b, b + r)],
        [pltpu.SemaphoreType.DMA((intervals, 2))],
        spec=HBM,
    )(propagator, forcing)
    other = swap(own)
    chip_map, *cuts = call(
        functools.partial(chip_kernel, heads),
        [(b, b)] + [(b // 2 + part, b)] * chips,
        [pltpu.VMEM((r, b), F32)],
    )(own, other)
    gathered = [
        lax.ppermute(cuts[d], "ry", filled([(h ^ d, h) for h in heads], chips)) for d in range(1, chips)
    ]
    swapped = [swap(value) for value in gathered]
    lineP, lineF, line_map, line_state = call(
        functools.partial(line_kernel, heads, chips),
        [(chips, b, b), (chips, part, b), (b, b), (part, b)],
    )(chip_map, cuts[0], *gathered, *swapped)

    def carried(value, width, pre):
        maps = [hop(value, d, 2 * width) for d in range(width, 2 * width)]
        if width == 1:
            return maps
        return call(functools.partial(prefix_map_kernel, width), [(b, b)])(*maps, *pre)

    total_map, total_state, pre_map, pre_state = line_map, line_state, [], None
    width, states = 1, []
    while width < lines:
        last = 2 * width >= lines
        if width > 1:
            total_state, *total_map = call(
                functools.partial(total_kernel, not last),
                [(part, b)] + [(b, b)] * (not last),
                flops=SHADOW,
            )(*pre_map * (not last), pre_state, line_map, line_state)
            total_map = total_map and total_map[0]
        states = [hop(total_state, d) for d in range(width, 2 * width)]
        if last:
            break
        pre_map = carried(total_map, width, pre_map)
        if width == 1:
            pre_state = states[0]
        else:
            (pre_state,) = call(functools.partial(prefix_state_kernel, width, width), [(part, b)])(
                *states, *pre_map, pre_state
            )
        width *= 2
    pre = [] if pre_state is None else [*pre_map, pre_state]
    first_late, _ = lax.optimization_barrier((first, line_state))
    following = lax.ppermute(first_late, ("rx", "ry"), [(i, (i - 1) % devices) for i in range(devices)])
    entering = call(
        functools.partial(enter_kernel, width, len(states), bool(pre)),
        [(part, b)] * chips,
        [pltpu.VMEM((part, b), F32)],
    )(*states, *pre, lineP, lineF)
    parts = [entering[0]] + [
        lax.ppermute(entering[d], "ry", filled([(h, h ^ d) for h in heads], chips)) for d in range(1, chips)
    ]
    return tuple(
        call(
            functools.partial(run_kernel, heads, chips),
            [(intervals, b, r)] * 2,
            [
                pltpu.VMEM((r, b), F32),
                pltpu.VMEM((intervals, b, r), F32),
                pltpu.VMEM((intervals, b, r), F32),
                pltpu.SemaphoreType.DMA((2, intervals)),
            ],
            out_spec=HBM,
        )(*parts, *[swap(value) for value in parts], other, following, first, rest)
    )


def solution(mesh):
    spec = P(("rx", "ry"), None, None)
    return jax.shard_map(
        on_device, mesh=mesh, in_specs=(spec, spec), out_specs=(spec, spec), check_vma=False
    )
```

```python
import functools

import jax
import jax.numpy as jnp
from jax import lax
from jax.experimental import pallas as pl
from jax.experimental.pallas import tpu as pltpu
from jax.sharding import PartitionSpec as P

F32 = jnp.float32
BF16 = jnp.bfloat16
NN = (((1,), (0,)), ((), ()))
VMEM = pl.BlockSpec(memory_space=pltpu.VMEM)
HBM = pl.BlockSpec(memory_space=pltpu.HBM)
SHADOW = 3_000_000_000


def split(value):
    high = value.astype(BF16)
    return high, (value - high.astype(F32)).astype(BF16)


def product(left, right):
    dot = functools.partial(lax.dot_general, dimension_numbers=NN, preferred_element_type=F32)
    return dot(left[0], right[0]) + (dot(left[0], right[1]) + dot(left[1], right[0]))


def call(kernel, outs, scratch=(), spec=VMEM, out_spec=VMEM, cost=0):
    shapes = [out if isinstance(out, jax.ShapeDtypeStruct) else jax.ShapeDtypeStruct(out, F32) for out in outs]

    def run(*args):
        specs = spec if isinstance(spec, list) else [spec] * len(args)
        return pl.pallas_call(
            kernel,
            in_specs=specs,
            out_specs=[out_spec] * len(outs),
            out_shape=shapes,
            scratch_shapes=list(scratch),
            cost_estimate=pl.CostEstimate(flops=cost, bytes_accessed=0, transcendentals=0) if cost else None,
            compiler_params=pltpu.CompilerParams(vmem_limit_bytes=32 * 1024 * 1024),
        )(*args)

    return run


def halved(*shape):
    return jax.ShapeDtypeStruct(shape, BF16)


def put(ref, value, *at):
    ref[*at, 0], ref[*at, 1] = split(value)


def get(ref, *at):
    return ref[*at, 0], ref[*at, 1]


def where():
    place = lax.axis_index("ry")
    return lax.axis_index("rx"), place // 2, place % 2


def rows(start, size):
    return pl.ds(pl.multiple_of(start, 8), size)


def local_kernel(a_ref, f_ref, own_ref, first_ref, rest_ref, sems):
    n, b = a_ref.shape[:2]
    copies = []
    for i in range(n):
        to = first_ref if i == 0 else rest_ref.at[i - 1]
        copies.append(
            (
                pltpu.make_async_copy(a_ref.at[i], to.at[:, pl.ds(0, b)], sems.at[i, 0]),
                pltpu.make_async_copy(f_ref.at[i], to.at[:, pl.ds(b, f_ref.shape[2])], sems.at[i, 1]),
            )
        )
    for part in range(2):
        for i in range(n):
            copies[i][part].start()
    copies[0][0].wait()
    total = first_ref[:, :b]
    steps = []
    for i in range(1, n):
        copies[i][0].wait()
        steps.append(split(rest_ref[i - 1, :, :b]))
        total = product(steps[-1], split(total))
    own_ref[:, :b] = total
    copies[0][1].wait()
    total = first_ref[:, b:]
    for i in range(1, n):
        copies[i][1].wait()
        total = product(steps[i - 1], split(total)) + rest_ref[i - 1, :, b:]
    own_ref[:, b:] = total


def chip_kernel(heads, own_ref, other_ref, map_ref, *refs):
    outs, state_ref = refs[:-1], refs[-1]
    _, z, core = where()
    b = own_ref.shape[0]
    part = outs[0].shape[0] - b // 2

    def combine(earlier_ref, later_ref):
        later = split(later_ref[:, :b])
        map_ref[...] = product(later, split(earlier_ref[:, :b])).T
        state_ref[...] = (product(later, split(earlier_ref[:, b:])) + later_ref[:, b:]).T

    @pl.when(core == 0)
    def _():
        combine(own_ref, other_ref)

    @pl.when(core == 1)
    def _():
        combine(other_ref, own_ref)

    for d, out in enumerate(outs):
        for j, head in enumerate(heads):

            @pl.when(z ^ d == head)
            def _():
                out[: b // 2] = map_ref[rows(core * (b // 2), b // 2)]
                out[b // 2 :] = state_ref[rows((2 * j + core) * part, part)]


def on_head(heads, body):
    pl.when(functools.reduce(jnp.logical_or, [where()[1] == head for head in heads]))(body)


def line_state_kernel(heads, chips, *refs):
    map_ref, ins, others = refs[0], refs[1 : 1 + chips], refs[1 + chips : 2 * chips]
    steps_ref, pre_ref, total_ref, all_ref = refs[2 * chips :]
    _, z, core = where()
    half = map_ref.shape[0] // 2

    def body():
        all_ref[z] = map_ref[...]
        for d in range(chips):
            pre_ref[z ^ d] = ins[d][half:]
            if d:
                all_ref[z ^ d, rows(core * half, half)] = ins[d][:half]
                all_ref[z ^ d, rows(half - core * half, half)] = others[d - 1][:half]
        total = pre_ref[0]
        for c in range(1, chips):
            here = pre_ref[c]
            pre_ref[c] = total
            put(steps_ref, all_ref[c], c)
            total = product(split(total), get(steps_ref, c)) + here
        total_ref[...] = total
        put(steps_ref, all_ref[0], 0)

    on_head(heads, body)


def line_map_kernel(heads, chips, steps_ref, pre_ref, total_ref):
    def body():
        pre_ref[1] = steps_ref[0]
        for c in range(1, chips):
            total = product(get(pre_ref, c), get(steps_ref, c))
            put(pre_ref, total, (c + 1) % chips)
        total_ref[...] = total

    if chips > 1:
        on_head(heads, body)
    else:
        pre_ref[...] = steps_ref[...]
        total_ref[...] = steps_ref[0, 0].astype(F32) + steps_ref[0, 1].astype(F32)


def total_kernel(with_map, *refs):
    *preP, preF_ref, line_ref, f_ref = refs[: 3 + with_map]
    outs = refs[3 + with_map :]
    step = get(line_ref, 0)
    outs[0][...] = product(split(preF_ref[...]), step) + f_ref[...]
    if with_map:
        outs[1][...] = product(split(preP[0][...]), step)


def choose(refs, width, out_ref):
    for j, ref in enumerate(refs):

        @pl.when(where()[0] % width == j)
        def _():
            out_ref[...] = ref[...]


def prefix_map_kernel(width, *refs):
    *maps, pre_ref, out_ref = refs
    g = where()[0]

    @pl.when(g // width % 2 == 0)
    def _():
        out_ref[...] = pre_ref[...]

    @pl.when(g // width % 2 == 1)
    def _():
        choose(maps, width, out_ref)

        @pl.when(g % width != 0)
        def _():
            out_ref[...] = product(split(out_ref[...]), split(pre_ref[...]))


def advance(width, states, pre, out_ref):
    g = where()[0]

    @pl.when(g // width % 2 == 1)
    def _():
        choose(states, width, out_ref)
        if pre:

            @pl.when(g % width != 0)
            def _():
                out_ref[...] = product(split(out_ref[...]), split(pre[0][...])) + pre[1][...]

    if pre:

        @pl.when(g // width % 2 == 0)
        def _():
            out_ref[...] = pre[1][...]


def prefix_state_kernel(width, count, *refs):
    advance(width, refs[:count], refs[count:-1], refs[-1])


def start_kernel(width, count, with_pre, ds, *refs):
    states, refs = refs[:count], refs[count:]
    pre, refs = refs[: 2 * with_pre], refs[2 * with_pre :]
    lineP_ref, lineF_ref, start_ref, *outs = refs
    if count:
        advance(width, states, pre, start_ref)

    @pl.when(where()[0] == 0)
    def _():
        start_ref[...] = jnp.zeros_like(start_ref)

    enter_kernel(ds, start_ref, lineP_ref, lineF_ref, *outs)


def enter_kernel(ds, start_ref, lineP_ref, lineF_ref, *outs):
    start = split(start_ref[...])
    for d, out in zip(ds, outs, strict=True):
        c = where()[1] ^ d

        @pl.when(c == 0)
        def _():
            out[...] = start_ref[...]

        @pl.when(c != 0)
        def _():
            out[...] = product(start, get(lineP_ref, c)) + lineF_ref[c]


def prepare_kernel(other_ref, first_ref, rest_ref, m_ref, c_ref, now_ref):
    core = where()[2]
    n, b = c_ref.shape[:2]

    @pl.when(core == 0)
    def _():
        now_ref[...] = first_ref[...]

    @pl.when(core == 1)
    def _():
        step = split(first_ref[:, :b])
        now_ref[:, :b] = product(step, split(other_ref[:, :b]))
        now_ref[:, b:] = product(step, split(other_ref[:, b:])) + first_ref[:, b:]

    for i in range(n):
        now = split(now_ref[...])
        m_ref[i, 0], m_ref[i, 1] = now[0][:, :b], now[1][:, :b]
        c_ref[i] = now_ref[:, b:]
        if i < n - 1:
            later = product(split(rest_ref[i, :, :b]), now)
            now_ref[:, :b] = later[:, :b]
            now_ref[:, b:] = later[:, b:] + rest_ref[i, :, b:]


def follow_kernel(m_ref, c_ref, next_ref, out_ref, add_ref):
    n, b = c_ref.shape[:2]
    step = split(next_ref[:, :b])
    put(out_ref, product(step, get(m_ref, n - 1)))
    add_ref[...] = product(step, split(c_ref[n - 1])) + next_ref[:, b:]


def run_kernel(heads, count, *refs):
    parts, shared = refs[:count], refs[count : 2 * count]
    m_ref, c_ref, next_ref, add_ref, x_ref, s_ref, in_ref, xs_ref, ss_ref, sems = refs[2 * count :]
    g, z, core = where()
    n = x_ref.shape[0]
    part = parts[0].shape[0]
    for d in range(count):
        for j, head in enumerate(heads):

            @pl.when(z ^ d == head)
            def _():
                in_ref[rows((2 * j + core) * part, part)] = parts[d][...]
                in_ref[rows((2 * j + 1 - core) * part, part)] = shared[d][...]

    entering = split(in_ref[...].T)
    copies = [pltpu.make_async_copy(xs_ref.at[i], x_ref.at[i], sems.at[0, i]) for i in range(n)]
    copies += [pltpu.make_async_copy(ss_ref.at[i], s_ref.at[i], sems.at[1, i]) for i in range(n)]
    for i in range(n):
        xs_ref[i] = product(get(m_ref, i), entering) + c_ref[i]
        copies[i].start()
        if i:
            ss_ref[i - 1] = xs_ref[i] - xs_ref[i - 1]
            copies[n + i - 1].start()
    ss_ref[n - 1] = product(get(next_ref), entering) + add_ref[...] - xs_ref[n - 1]

    @pl.when(g * lax.axis_size("ry") + 2 * z + core == lax.axis_size("rx") * lax.axis_size("ry") - 1)
    def _():
        ss_ref[n - 1] = -xs_ref[n - 1]

    copies[2 * n - 1].start()
    for copy in copies:
        copy.wait()


def filled(useful, chips):
    sources = [c for c in range(chips) if all(c != s for s, _ in useful)]
    targets = [c for c in range(chips) if all(c != t for _, t in useful)]
    pairs = []
    for s, t in [*useful, *zip(sources, targets, strict=True)]:
        pairs += [(2 * s + core, 2 * t + (core ^ (s == t))) for core in range(2)]
    return pairs


def on_device(propagator, forcing):
    intervals, b, r = forcing.shape
    lines, places = lax.axis_size("rx"), lax.axis_size("ry")
    chips, devices = places // 2, lines * places
    heads = sorted({max(chips // 2 - 1, 0), chips // 2})
    part = r // (2 * len(heads))

    def swap(value):
        return lax.ppermute(value, "ry", [(i, i ^ 1) for i in range(places)])

    def to_heads(value, d):
        return lax.ppermute(value, "ry", filled([(h ^ d, h) for h in heads], chips))

    def from_heads(value, d):
        return lax.ppermute(value, "ry", filled([(h, h ^ d) for h in heads], chips))

    def hops(value, width, start=0):
        out = []
        for j in range(width):
            to = {}
            for block in range(start, lines, 2 * width):
                source, target = block + width - 1, block + width + j
                back = block + j
                to[source], to[target], to[back] = target, back, source
                if back == source:
                    to[source] = target
            pairs = []
            for g in range(lines):
                for i in range(places):
                    at = to.get(g) if i // 2 in heads else None
                    pairs.append((g * places + i, g * places + (i ^ 1) if at is None else at * places + i))
            out.append(lax.ppermute(value, ("rx", "ry"), pairs))
        return out

    propagator, forcing = (pltpu.with_memory_space_constraint(a, pltpu.HBM) for a in (propagator, forcing))
    own, first, rest = call(
        local_kernel,
        [(b, b + r), (b, b + r), (max(intervals - 1, 1), b, b + r)],
        [pltpu.SemaphoreType.DMA((intervals, 2))],
        spec=HBM,
    )(propagator, forcing)
    other = swap(own)
    chip_map, *cuts = call(
        functools.partial(chip_kernel, heads),
        [(b, b)] + [(b // 2 + part, b)] * chips,
        [pltpu.VMEM((r, b), F32)],
    )(own, other)
    gathered = [to_heads(cuts[d], d) for d in range(1, chips)]
    early, _ = lax.optimization_barrier((first, cuts))
    matrices, constants = call(
        prepare_kernel,
        [halved(intervals, 2, b, b), (intervals, b, r)],
        [pltpu.VMEM((b, b + r), F32)],
        cost=SHADOW,
    )(other, early, rest)
    for d in range(chips - 1):
        gathered[d], _ = lax.optimization_barrier((gathered[d], constants))
    swapped = [swap(value) for value in gathered]
    steps, lineF, line_state = call(
        functools.partial(line_state_kernel, heads, chips),
        [halved(chips, 2, b, b), (chips, part, b), (part, b)],
        [pltpu.VMEM((chips, b, b), F32)],
    )(chip_map, cuts[0], *gathered, *swapped)
    lineP, line_map = call(
        functools.partial(line_map_kernel, heads, chips), [halved(chips, 2, b, b), (b, b)], cost=SHADOW
    )(steps)

    def carried(value, width, pre):
        maps = hops(value, width, 2 * width)
        if width == 1:
            return maps
        return call(functools.partial(prefix_map_kernel, width), [(b, b)])(*maps, *pre)

    total_map, total_state, pre_map, pre_state = line_map, line_state, [], None
    width, states = 1, []
    while width < lines:
        last = 2 * width >= lines
        if width > 1:
            total_state, *more = call(
                functools.partial(total_kernel, not last), [(part, b)] + [(b, b)] * (not last), cost=SHADOW
            )(*pre_map * (not last), pre_state, lineP, line_state)
            total_map = more and more[0]
        states = hops(total_state, width)
        if last:
            break
        pre_map = carried(total_map, width, pre_map)
        if width == 1:
            pre_state = states[0]
        else:
            (pre_state,) = call(functools.partial(prefix_state_kernel, width, width), [(part, b)])(
                *states, *pre_map, pre_state
            )
        width *= 2
    pre = [] if pre_state is None else [*pre_map, pre_state]
    first_late, _ = lax.optimization_barrier((first, line_state))
    following = lax.ppermute(first_late, ("rx", "ry"), [(i, (i - 1) % devices) for i in range(devices)])
    near, far = range(max(chips // 2, 1)), range(max(chips // 2, 1), chips)
    start, *later = call(
        functools.partial(start_kernel, width, len(states), bool(pre), far), [(part, b)] * (1 + len(far))
    )(*states, *pre, lineP, lineF)
    entering = call(functools.partial(enter_kernel, near), [(part, b)] * len(near), cost=SHADOW)(start, lineP, lineF)
    entering = [*entering, *later]
    parts = [entering[0]] + [from_heads(entering[d], d) for d in range(1, chips)]
    following, _ = lax.optimization_barrier((following, start))
    next_matrix, next_constant = call(follow_kernel, [halved(2, b, b), (b, r)], cost=SHADOW)(
        matrices, constants, following
    )
    for d in range(1, chips):
        parts[d], _ = lax.optimization_barrier((parts[d], next_constant))
    return tuple(
        call(
            functools.partial(run_kernel, heads, chips),
            [(intervals, b, r)] * 2,
            [
                pltpu.VMEM((r, b), F32),
                pltpu.VMEM((intervals, b, r), F32),
                pltpu.VMEM((intervals, b, r), F32),
                pltpu.SemaphoreType.DMA((2, intervals)),
            ],
            out_spec=HBM,
        )(*parts, *[swap(value) for value in parts], matrices, constants, next_matrix, next_constant)
    )


def solution(mesh):
    spec = P(("rx", "ry"), None, None)
    return jax.shard_map(
        on_device, mesh=mesh, in_specs=(spec, spec), out_specs=(spec, spec), check_vma=False
    )
```

```python
import functools

import jax
import jax.numpy as jnp
from jax import lax
from jax.experimental import pallas as pl
from jax.experimental.pallas import tpu as pltpu
from jax.sharding import PartitionSpec as P

F32 = jnp.float32
BF16 = jnp.bfloat16
NN = (((1,), (0,)), ((), ()))
NT = (((1,), (1,)), ((), ()))
VMEM = pl.BlockSpec(memory_space=pltpu.VMEM)
HBM = pl.BlockSpec(memory_space=pltpu.HBM)
SHADOW = 3_000_000_000


def split(value):
    high = value.astype(BF16)
    return high, (value - high.astype(F32)).astype(BF16)


def product(left, right, dims=NN):
    dot = functools.partial(lax.dot_general, dimension_numbers=dims, preferred_element_type=F32)
    return dot(left[0], right[0]) + (dot(left[0], right[1]) + dot(left[1], right[0]))


def call(kernel, outs, scratch=(), spec=VMEM, out_spec=VMEM, cost=0):
    shapes = [out if isinstance(out, jax.ShapeDtypeStruct) else jax.ShapeDtypeStruct(out, F32) for out in outs]

    def run(*args):
        specs = spec if isinstance(spec, list) else [spec] * len(args)
        return pl.pallas_call(
            kernel,
            in_specs=specs,
            out_specs=[out_spec] * len(outs),
            out_shape=shapes,
            scratch_shapes=list(scratch),
            cost_estimate=pl.CostEstimate(flops=cost, bytes_accessed=0, transcendentals=0) if cost else None,
            compiler_params=pltpu.CompilerParams(vmem_limit_bytes=32 * 1024 * 1024),
        )(*args)

    return run


def halved(*shape):
    return jax.ShapeDtypeStruct(shape, BF16)


def put(ref, value, *at):
    ref[*at, 0], ref[*at, 1] = split(value)


def get(ref, *at):
    return ref[*at, 0], ref[*at, 1]


def where():
    place = lax.axis_index("ry")
    return lax.axis_index("rx"), place // 2, place % 2


def rows(start, size):
    return pl.ds(pl.multiple_of(start, 8), size)


def local_kernel(a_ref, f_ref, own_ref, first_ref, rest_ref, sems):
    n, b = a_ref.shape[:2]
    copies = []
    for i in range(n):
        to = first_ref if i == 0 else rest_ref.at[i - 1]
        copies.append(
            (
                pltpu.make_async_copy(a_ref.at[i], to.at[:, pl.ds(0, b)], sems.at[i, 0]),
                pltpu.make_async_copy(f_ref.at[i], to.at[:, pl.ds(b, f_ref.shape[2])], sems.at[i, 1]),
            )
        )
    for part in range(2):
        for i in range(n):
            copies[i][part].start()
    copies[0][0].wait()
    total = first_ref[:, :b]
    steps = []
    for i in range(1, n):
        copies[i][0].wait()
        steps.append(split(rest_ref[i - 1, :, :b]))
        total = product(steps[-1], split(total))
    own_ref[:, :b] = total
    copies[0][1].wait()
    total = first_ref[:, b:]
    for i in range(1, n):
        copies[i][1].wait()
        total = product(steps[i - 1], split(total)) + rest_ref[i - 1, :, b:]
    own_ref[:, b:] = total


def chip_kernel(heads, ds, own_ref, other_ref, map_ref, state_ref, *outs):
    core = where()[2]
    b = own_ref.shape[0]

    def combine(earlier_ref, later_ref):
        later = split(later_ref[:, :b])
        map_ref[...] = product(later, split(earlier_ref[:, :b])).T
        state_ref[...] = (product(later, split(earlier_ref[:, b:])) + later_ref[:, b:]).T

    @pl.when(core == 0)
    def _():
        combine(own_ref, other_ref)

    @pl.when(core == 1)
    def _():
        combine(other_ref, own_ref)

    cut_kernel(heads, ds, map_ref, state_ref, *outs)


def cut_kernel(heads, ds, map_ref, state_ref, *outs):
    _, z, core = where()
    half = map_ref.shape[0] // 2
    part = outs[0].shape[0] - half
    for d, out in zip(ds, outs, strict=True):
        for j, head in enumerate(heads):

            @pl.when(z ^ d == head)
            def _():
                out[:half] = map_ref[rows(core * half, half)]
                out[half:] = state_ref[rows((2 * j + core) * part, part)]


def on_head(heads, body):
    pl.when(functools.reduce(jnp.logical_or, [where()[1] == head for head in heads]))(body)


def line_state_kernel(heads, chips, *refs):
    map_ref, ins, others = refs[0], refs[1 : 1 + chips], refs[1 + chips : 2 * chips]
    steps_ref, pre_ref, total_ref, all_ref = refs[2 * chips :]
    _, z, core = where()
    half = map_ref.shape[0] // 2

    def body():
        all_ref[z] = map_ref[...]
        for d in range(chips):
            pre_ref[z ^ d] = ins[d][half:]
            if d:
                all_ref[z ^ d, rows(core * half, half)] = ins[d][:half]
                all_ref[z ^ d, rows(half - core * half, half)] = others[d - 1][:half]
        total = pre_ref[0]
        for c in range(1, chips):
            here = pre_ref[c]
            pre_ref[c] = total
            put(steps_ref, all_ref[c], c)
            total = product(split(total), get(steps_ref, c)) + here
        total_ref[...] = total
        put(steps_ref, all_ref[0], 0)

    on_head(heads, body)


def line_map_kernel(heads, chips, steps_ref, state_ref, pre_ref, total_ref):
    b = steps_ref.shape[2]

    def body():
        if chips == 1:
            pre_ref[0] = steps_ref[0]
            total_ref[:b] = steps_ref[0, 0].astype(F32) + steps_ref[0, 1].astype(F32)
        else:
            pre_ref[1] = steps_ref[0]
        for c in range(1, chips):
            total = product(get(pre_ref, c), get(steps_ref, c))
            put(pre_ref, total, (c + 1) % chips)
            if c == chips - 1:
                total_ref[:b] = total
        total_ref[b:] = state_ref[...]

    on_head(heads, body)


def total_kernel(whole, *refs):
    pre0_ref, *pre, line_ref, f_ref = refs[: 3 + whole]
    outs = refs[3 + whole :]
    b = line_ref.shape[2]
    step = get(line_ref, 0)
    outs[0][...] = product(split(pre0_ref[...]), step) + f_ref[...]
    if whole:
        total = product(split(pre[0][...]), step)
        outs[1][:b] = total[:b]
        outs[1][b:] = total[b:] + f_ref[...]


def choose(refs, width, out_ref):
    for j, ref in enumerate(refs):

        @pl.when(where()[0] % width == j)
        def _():
            out_ref[...] = ref[...]


def advance(width, states, pre0, pre, out_ref):
    g = where()[0]

    @pl.when(g // width % 2 == 1)
    def _():
        choose(states, width, out_ref)
        if pre:
            b = out_ref.shape[1]

            @pl.when(g % width != 0)
            def _():
                out_ref[...] = product(split(out_ref[...]), split(pre[0][:b])) + pre[0][b:]

    if pre0:

        @pl.when(g // width % 2 == 0)
        def _():
            out_ref[...] = pre0[0][...]


def prefix_kernel(width, *refs):
    states, maps, (pre0_ref, pre_ref, out0_ref, out_ref) = refs[:width], refs[width : 2 * width], refs[2 * width :]
    g = where()[0]
    b = pre_ref.shape[1]
    advance(width, states, [pre0_ref], [pre_ref], out0_ref)

    @pl.when(g // width % 2 == 0)
    def _():
        out_ref[...] = pre_ref[...]

    @pl.when(g // width % 2 == 1)
    def _():
        choose(maps, width, out_ref)

        @pl.when(g % width != 0)
        def _():
            out_ref[...] = product(split(out_ref[...]), split(pre_ref[:b]))
            out_ref[b:] += pre_ref[b:]


def start_kernel(width, count, with_pre, ds, *refs):
    states, refs = refs[:count], refs[count:]
    pre, refs = refs[: 2 * with_pre], refs[2 * with_pre :]
    lineP_ref, lineF_ref, start_ref, *outs = refs
    if count:
        advance(width, states, pre[:1], pre[1:], start_ref)

    @pl.when(where()[0] == 0)
    def _():
        start_ref[...] = jnp.zeros_like(start_ref)

    enter_kernel(ds, start_ref, lineP_ref, lineF_ref, *outs)


def enter_kernel(ds, start_ref, lineP_ref, lineF_ref, *outs):
    start = split(start_ref[...])
    for d, out in zip(ds, outs, strict=True):
        c = where()[1] ^ d

        @pl.when(c == 0)
        def _():
            out[...] = start_ref[...]

        @pl.when(c != 0)
        def _():
            out[...] = product(start, get(lineP_ref, c)) + lineF_ref[c]


def prepare_kernel(other_ref, first_ref, rest_ref, m_ref, c_ref, now_ref):
    core = where()[2]
    n, b = c_ref.shape[:2]

    @pl.when(core == 0)
    def _():
        now_ref[...] = first_ref[...]

    @pl.when(core == 1)
    def _():
        step = split(first_ref[:, :b])
        now_ref[:, :b] = product(step, split(other_ref[:, :b]))
        now_ref[:, b:] = product(step, split(other_ref[:, b:])) + first_ref[:, b:]

    for i in range(n):
        now = split(now_ref[...])
        m_ref[i, 0], m_ref[i, 1] = now[0][:, :b], now[1][:, :b]
        c_ref[i] = now_ref[:, b:]
        if i < n - 1:
            later = product(split(rest_ref[i, :, :b]), now)
            now_ref[:, :b] = later[:, :b]
            now_ref[:, b:] = later[:, b:] + rest_ref[i, :, b:]


def follow_kernel(m_ref, c_ref, next_ref, out_ref, add_ref):
    n, b = c_ref.shape[:2]
    step = split(next_ref[:, :b])
    put(out_ref, product(step, get(m_ref, n - 1)))
    add_ref[...] = product(step, split(c_ref[n - 1])) + next_ref[:, b:]


def run_kernel(heads, count, *refs):
    parts, shared = refs[:count], refs[count : 2 * count]
    m_ref, c_ref, next_ref, add_ref, x_ref, s_ref, in_ref, xs_ref, ss_ref, sems = refs[2 * count :]
    g, z, core = where()
    n = x_ref.shape[0]
    part = parts[0].shape[0]
    for d in range(count):
        for j, head in enumerate(heads):

            @pl.when(z ^ d == head)
            def _():
                in_ref[rows((2 * j + core) * part, part)] = parts[d][...]
                in_ref[rows((2 * j + 1 - core) * part, part)] = shared[d][...]

    entering = split(in_ref[...])
    copies = [pltpu.make_async_copy(xs_ref.at[i], x_ref.at[i], sems.at[0, i]) for i in range(n)]
    copies += [pltpu.make_async_copy(ss_ref.at[i], s_ref.at[i], sems.at[1, i]) for i in range(n)]
    for i in range(n):
        xs_ref[i] = product(get(m_ref, i), entering, NT) + c_ref[i]
        copies[i].start()
        if i:
            ss_ref[i - 1] = xs_ref[i] - xs_ref[i - 1]
            copies[n + i - 1].start()
    ss_ref[n - 1] = product(get(next_ref), entering, NT) + add_ref[...] - xs_ref[n - 1]

    @pl.when(g * lax.axis_size("ry") + 2 * z + core == lax.axis_size("rx") * lax.axis_size("ry") - 1)
    def _():
        ss_ref[n - 1] = -xs_ref[n - 1]

    copies[2 * n - 1].start()
    for copy in copies:
        copy.wait()


def filled(useful, chips):
    sources = [c for c in range(chips) if all(c != s for s, _ in useful)]
    targets = [c for c in range(chips) if all(c != t for _, t in useful)]
    pairs = []
    for s, t in [*useful, *zip(sources, targets, strict=True)]:
        pairs += [(2 * s + core, 2 * t + (core ^ (s == t))) for core in range(2)]
    return pairs


def on_device(propagator, forcing):
    intervals, b, r = forcing.shape
    lines, places = lax.axis_size("rx"), lax.axis_size("ry")
    chips, devices = places // 2, lines * places
    heads = sorted({max(chips // 2 - 1, 0), chips // 2})
    part = r // (2 * len(heads))

    def swap(value):
        return lax.ppermute(value, "ry", [(i, i ^ 1) for i in range(places)])

    def to_heads(value, d):
        return lax.ppermute(value, "ry", filled([(h ^ d, h) for h in heads], chips))

    def from_heads(value, d):
        return lax.ppermute(value, "ry", filled([(h, h ^ d) for h in heads], chips))

    def hops(value, width, first=True):
        out = []
        for j in range(width):
            to = {}
            for block in range(0 if first else 2 * width, 2 * width if first else lines, 2 * width):
                source, target = block + width - 1, block + width + j
                back = block + j if j < width - 1 else target
                to[source], to[target] = target, source
                if back != target:
                    to[target], to[back] = back, source
            pairs = []
            for g in range(lines):
                for i in range(places):
                    at = to.get(g) if i // 2 in heads else None
                    pairs.append((g * places + i, g * places + (i ^ 1) if at is None else at * places + i))
            out.append(lax.ppermute(value, ("rx", "ry"), pairs))
        return out

    propagator, forcing = (pltpu.with_memory_space_constraint(a, pltpu.HBM) for a in (propagator, forcing))
    own, first, rest = call(
        local_kernel,
        [(b, b + r), (b, b + r), (max(intervals - 1, 1), b, b + r)],
        [pltpu.SemaphoreType.DMA((intervals, 2))],
        spec=HBM,
    )(propagator, forcing)
    other = swap(own)
    soon = [d for d in range(chips) if chips // 2 <= d < max(chips - 1, 1)]
    later = [d for d in range(chips) if d not in soon]
    chip_map, chip_state, *cuts = call(
        functools.partial(chip_kernel, heads, soon), [(b, b), (r, b)] + [(b // 2 + part, b)] * len(soon)
    )(own, other)
    more = call(functools.partial(cut_kernel, heads, later), [(b // 2 + part, b)] * len(later), cost=SHADOW)(
        chip_map, chip_state
    )
    cuts = dict(zip([*soon, *later], [*cuts, *more], strict=True))
    gathered = [to_heads(cuts[d], d) for d in range(1, chips)]
    early, _ = lax.optimization_barrier((first, cuts[0]))
    matrices, constants = call(
        prepare_kernel,
        [halved(intervals, 2, b, b), (intervals, b, r)],
        [pltpu.VMEM((b, b + r), F32)],
        cost=SHADOW,
    )(other, early, rest)
    for d in range(chips - 1):
        gathered[d], _ = lax.optimization_barrier((gathered[d], constants))
    swapped = [swap(value) for value in gathered]
    first_late, _ = lax.optimization_barrier((first, gathered))
    following = lax.ppermute(first_late, ("rx", "ry"), [(i, (i - 1) % devices) for i in range(devices)])
    steps, lineF, line_state = call(
        functools.partial(line_state_kernel, heads, chips),
        [halved(chips, 2, b, b), (chips, part, b), (part, b)],
        [pltpu.VMEM((chips, b, b), F32)],
    )(chip_map, cuts[0], *gathered, *swapped)
    lineP, line_map = call(
        functools.partial(line_map_kernel, heads, chips), [halved(chips, 2, b, b), (b + part, b)], cost=SHADOW
    )(steps, line_state)

    total_map, total_state, pre = line_map, line_state, []
    width, states = 1, []
    while width < lines:
        last = 2 * width >= lines
        if width > 1:
            total_state, *more = call(
                functools.partial(total_kernel, not last), [(part, b)] + [(b + part, b)] * (not last), cost=SHADOW
            )(*pre[: 2 - last], lineP, line_state)
            total_map = more and more[0]
        states = hops(total_state, width)
        if last:
            break
        maps = hops(total_map, width, first=False)
        if width == 1:
            pre = [*states, *maps]
        else:
            pre = call(functools.partial(prefix_kernel, width), [(part, b), (b + part, b)])(*states, *maps, *pre)
        width *= 2
    near, far = range(max(chips // 2, 1)), range(max(chips // 2, 1), chips)
    start, *later = call(
        functools.partial(start_kernel, width, len(states), bool(pre), far), [(part, b)] * (1 + len(far))
    )(*states, *pre, lineP, lineF)
    entering = call(functools.partial(enter_kernel, near), [(part, b)] * len(near), cost=SHADOW)(start, lineP, lineF)
    entering = [*entering, *later]
    parts = [entering[0]] + [from_heads(entering[d], d) for d in range(1, chips)]
    following, _ = lax.optimization_barrier((following, start))
    next_matrix, next_constant = call(follow_kernel, [halved(2, b, b), (b, r)], cost=SHADOW)(
        matrices, constants, following
    )
    for d in range(1, chips):
        parts[d], _ = lax.optimization_barrier((parts[d], next_constant))
    shared = {d: swap(parts[d]) for d in range(chips) if d != 1}
    if chips > 1:
        parts[1], shared = lax.optimization_barrier((parts[1], shared))
        shared[1] = swap(parts[1])
    return tuple(
        call(
            functools.partial(run_kernel, heads, chips),
            [(intervals, b, r)] * 2,
            [
                pltpu.VMEM((r, b), F32),
                pltpu.VMEM((intervals, b, r), F32),
                pltpu.VMEM((intervals, b, r), F32),
                pltpu.SemaphoreType.DMA((2, intervals)),
            ],
            out_spec=HBM,
        )(*parts, *[shared[d] for d in range(chips)], matrices, constants, next_matrix, next_constant)
    )


def solution(mesh):
    spec = P(("rx", "ry"), None, None)
    return jax.shard_map(
        on_device, mesh=mesh, in_specs=(spec, spec), out_specs=(spec, spec), check_vma=False
    )
```

```python
import functools

import jax
import jax.numpy as jnp
from jax import lax
from jax.experimental import pallas as pl
from jax.experimental.pallas import tpu as pltpu
from jax.sharding import PartitionSpec as P

F32 = jnp.float32
BF16 = jnp.bfloat16
NN = (((1,), (0,)), ((), ()))
NT = (((1,), (1,)), ((), ()))
VMEM = pl.BlockSpec(memory_space=pltpu.VMEM)
HBM = pl.BlockSpec(memory_space=pltpu.HBM)
SHADOW = 3_000_000_000


def split(value):
    high = value.astype(BF16)
    return high, (value - high.astype(F32)).astype(BF16)


def product(left, right, dims=NN):
    dot = functools.partial(lax.dot_general, dimension_numbers=dims, preferred_element_type=F32)
    return dot(left[0], right[0]) + (dot(left[0], right[1]) + dot(left[1], right[0]))


def call(kernel, outs, scratch=(), spec=VMEM, out_spec=VMEM, cost=0):
    shapes = [out if isinstance(out, jax.ShapeDtypeStruct) else jax.ShapeDtypeStruct(out, F32) for out in outs]

    def run(*args):
        specs = spec if isinstance(spec, list) else [spec] * len(args)
        return pl.pallas_call(
            kernel,
            in_specs=specs,
            out_specs=[out_spec] * len(outs),
            out_shape=shapes,
            scratch_shapes=list(scratch),
            cost_estimate=pl.CostEstimate(flops=cost, bytes_accessed=0, transcendentals=0) if cost else None,
            compiler_params=pltpu.CompilerParams(vmem_limit_bytes=32 * 1024 * 1024),
        )(*args)

    return run


def halved(*shape):
    return jax.ShapeDtypeStruct(shape, BF16)


def put(ref, value, *at):
    ref[*at, 0], ref[*at, 1] = split(value)


def get(ref, *at):
    return ref[*at, 0], ref[*at, 1]


def where():
    place = lax.axis_index("ry")
    return lax.axis_index("rx"), place // 2, place % 2


def rows(start, size):
    return pl.ds(pl.multiple_of(start, 8), size)


def local_kernel(a_ref, f_ref, own_ref, first_ref, rest_ref, sems):
    n, b = a_ref.shape[:2]
    copies = []
    for i in range(n):
        to = first_ref if i == 0 else rest_ref.at[i - 1]
        copies.append(
            (
                pltpu.make_async_copy(a_ref.at[i], to.at[:, pl.ds(0, b)], sems.at[i, 0]),
                pltpu.make_async_copy(f_ref.at[i], to.at[:, pl.ds(b, f_ref.shape[2])], sems.at[i, 1]),
            )
        )
    for part in range(2):
        for i in range(n):
            copies[i][part].start()
    copies[0][0].wait()
    total = first_ref[:, :b]
    steps = []
    for i in range(1, n):
        copies[i][0].wait()
        steps.append(split(rest_ref[i - 1, :, :b]))
        total = product(steps[-1], split(total))
    own_ref[:, :b] = total
    copies[0][1].wait()
    total = first_ref[:, b:]
    for i in range(1, n):
        copies[i][1].wait()
        total = product(steps[i - 1], split(total)) + rest_ref[i - 1, :, b:]
    own_ref[:, b:] = total


def chip_kernel(heads, ds, own_ref, other_ref, map_ref, state_ref, *outs):
    core = where()[2]
    b = own_ref.shape[0]

    def combine(earlier_ref, later_ref):
        later = split(later_ref[:, :b])
        map_ref[...] = product(later, split(earlier_ref[:, :b])).T
        state_ref[...] = (product(later, split(earlier_ref[:, b:])) + later_ref[:, b:]).T

    @pl.when(core == 0)
    def _():
        combine(own_ref, other_ref)

    @pl.when(core == 1)
    def _():
        combine(other_ref, own_ref)

    cut_kernel(heads, ds, map_ref, state_ref, *outs)


def cut_kernel(heads, ds, map_ref, state_ref, *outs):
    _, z, core = where()
    half = map_ref.shape[0] // 2
    part = outs[0].shape[0] - half
    for d, out in zip(ds, outs, strict=True):
        for j, head in enumerate(heads):

            @pl.when(z ^ d == head)
            def _():
                out[:half] = map_ref[rows(core * half, half)]
                out[half:] = state_ref[rows((2 * j + core) * part, part)]


def on_head(heads, body):
    pl.when(functools.reduce(jnp.logical_or, [where()[1] == head for head in heads]))(body)


def line_state_kernel(heads, chips, *refs):
    map_ref, ins, others = refs[0], refs[1 : 1 + chips], refs[1 + chips : 2 * chips]
    steps_ref, pre_ref, total_ref, all_ref = refs[2 * chips :]
    _, z, core = where()
    half = map_ref.shape[0] // 2

    def body():
        all_ref[z] = map_ref[...]
        for d in range(chips):
            pre_ref[z ^ d] = ins[d][half:]
            if d:
                all_ref[z ^ d, rows(core * half, half)] = ins[d][:half]
                all_ref[z ^ d, rows(half - core * half, half)] = others[d - 1][:half]
        total = pre_ref[0]
        for c in range(1, chips):
            here = pre_ref[c]
            pre_ref[c] = total
            put(steps_ref, all_ref[c], c)
            total = product(split(total), get(steps_ref, c)) + here
        total_ref[...] = total
        put(steps_ref, all_ref[0], 0)

    on_head(heads, body)


def line_map_kernel(heads, chips, steps_ref, state_ref, pre_ref, total_ref, all_ref):
    half = steps_ref.shape[2] // 2

    def body():
        pre_ref[1 % chips] = steps_ref[0]
        total = steps_ref[0, 0].astype(F32) + steps_ref[0, 1].astype(F32)
        for c in range(1, chips):
            total = product(get(pre_ref, c), get(steps_ref, c))
            put(pre_ref, total, (c + 1) % chips)
        all_ref[...] = total
        total_ref[:half] = all_ref[rows(where()[2] * half, half)]
        total_ref[half:] = state_ref[...]

    on_head(heads, body)


def total_kernel(whole, *refs):
    pre0_ref, *pre, line_ref, f_ref = refs[: 3 + whole]
    outs = refs[3 + whole :]
    b = line_ref.shape[2]
    step = get(line_ref, 0)
    outs[0][...] = product(split(pre0_ref[...]), step) + f_ref[...]
    if whole:
        half = b // 2
        outs[2][...] = product(split(pre[0][:b]), step)
        outs[1][:half] = outs[2][rows(where()[2] * half, half)]
        outs[1][half:] = product(split(pre[0][b:]), step) + f_ref[...]


def choose(refs, width, out_ref):
    for j, ref in enumerate(refs):

        @pl.when(where()[0] % width == j)
        def _():
            out_ref[...] = ref[...]


def advance(width, states, pre0, pre, out_ref):
    g = where()[0]

    @pl.when(g // width % 2 == 1)
    def _():
        choose(states, width, out_ref)
        if pre:
            b = out_ref.shape[1]

            @pl.when(g % width != 0)
            def _():
                out_ref[...] = product(split(out_ref[...]), split(pre[0][:b])) + pre[0][b:]

    if pre0:

        @pl.when(g // width % 2 == 0)
        def _():
            out_ref[...] = pre0[0][...]


def pieces_kernel(in_ref, *outs):
    size = outs[0].shape[0]
    for i, out in enumerate(outs):
        out[...] = in_ref[i * size : (i + 1) * size]


def whole_kernel(own_ref, *refs):
    others, out_ref = refs[:-1], refs[-1]
    core = where()[2]
    b = out_ref.shape[1]
    half, size = b // 2, b // 2 // len(others)
    out_ref[rows(core * half, half)] = own_ref[:half]
    for i, other_ref in enumerate(others):
        out_ref[rows(half - core * half + i * size, size)] = other_ref[:size]
    out_ref[b:] = own_ref[half:]


def prefix_kernel(width, *refs):
    states, maps, (pre0_ref, pre_ref, out0_ref, out_ref) = refs[:width], refs[width : 2 * width], refs[2 * width :]
    g = where()[0]
    b = pre_ref.shape[1]
    advance(width, states, [pre0_ref], [pre_ref], out0_ref)

    @pl.when(g // width % 2 == 0)
    def _():
        out_ref[...] = pre_ref[...]

    @pl.when(g // width % 2 == 1)
    def _():
        choose(maps, width, out_ref)

        @pl.when(g % width != 0)
        def _():
            out_ref[...] = product(split(out_ref[...]), split(pre_ref[:b]))
            out_ref[b:] += pre_ref[b:]


def start_kernel(width, count, with_pre, ds, *refs):
    states, refs = refs[:count], refs[count:]
    pre, refs = refs[:with_pre], refs[with_pre:]
    lineP_ref, lineF_ref, start_ref, *outs, pre_ref = refs
    if with_pre > 2:
        whole_kernel(*pre[1:], pre_ref)
    if count:
        advance(width, states, pre[:1], [pre_ref] if with_pre > 2 else pre[1:], start_ref)

    @pl.when(where()[0] == 0)
    def _():
        start_ref[...] = jnp.zeros_like(start_ref)

    enter_kernel(ds, start_ref, lineP_ref, lineF_ref, *outs)


def enter_kernel(ds, start_ref, lineP_ref, lineF_ref, *outs):
    start = split(start_ref[...])
    for d, out in zip(ds, outs, strict=True):
        c = where()[1] ^ d

        @pl.when(c == 0)
        def _():
            out[...] = start_ref[...]

        @pl.when(c != 0)
        def _():
            out[...] = product(start, get(lineP_ref, c)) + lineF_ref[c]


def prepare_kernel(other_ref, first_ref, rest_ref, m_ref, c_ref, now_ref):
    core = where()[2]
    n, b = c_ref.shape[:2]

    @pl.when(core == 0)
    def _():
        now_ref[...] = first_ref[...]

    @pl.when(core == 1)
    def _():
        step = split(first_ref[:, :b])
        now_ref[:, :b] = product(step, split(other_ref[:, :b]))
        now_ref[:, b:] = product(step, split(other_ref[:, b:])) + first_ref[:, b:]

    for i in range(n):
        now = split(now_ref[...])
        m_ref[i, 0], m_ref[i, 1] = now[0][:, :b], now[1][:, :b]
        c_ref[i] = now_ref[:, b:]
        if i < n - 1:
            later = product(split(rest_ref[i, :, :b]), now)
            now_ref[:, :b] = later[:, :b]
            now_ref[:, b:] = later[:, b:] + rest_ref[i, :, b:]


def follow_kernel(m_ref, c_ref, next_ref, out_ref, add_ref):
    n, b = c_ref.shape[:2]
    step = split(next_ref[:, :b])
    put(out_ref, product(step, get(m_ref, n - 1)))
    add_ref[...] = product(step, split(c_ref[n - 1])) + next_ref[:, b:]


def run_kernel(heads, count, *refs):
    parts, shared = refs[:count], refs[count : 2 * count]
    m_ref, c_ref, next_ref, add_ref, x_ref, s_ref, in_ref, xs_ref, ss_ref, sems = refs[2 * count :]
    g, z, core = where()
    n = x_ref.shape[0]
    part = parts[0].shape[0]
    for d in range(count):
        for j, head in enumerate(heads):

            @pl.when(z ^ d == head)
            def _():
                in_ref[rows((2 * j + core) * part, part)] = parts[d][...]
                in_ref[rows((2 * j + 1 - core) * part, part)] = shared[d][...]

    entering = split(in_ref[...])
    copies = [pltpu.make_async_copy(xs_ref.at[i], x_ref.at[i], sems.at[0, i]) for i in range(n)]
    copies += [pltpu.make_async_copy(ss_ref.at[i], s_ref.at[i], sems.at[1, i]) for i in range(n)]
    for i in range(n):
        xs_ref[i] = product(get(m_ref, i), entering, NT) + c_ref[i]
        copies[i].start()
        if i:
            ss_ref[i - 1] = xs_ref[i] - xs_ref[i - 1]
            copies[n + i - 1].start()
    ss_ref[n - 1] = product(get(next_ref), entering, NT) + add_ref[...] - xs_ref[n - 1]

    @pl.when(g * lax.axis_size("ry") + 2 * z + core == lax.axis_size("rx") * lax.axis_size("ry") - 1)
    def _():
        ss_ref[n - 1] = -xs_ref[n - 1]

    copies[2 * n - 1].start()
    for copy in copies:
        copy.wait()


def filled(useful, chips):
    sources = [c for c in range(chips) if all(c != s for s, _ in useful)]
    targets = [c for c in range(chips) if all(c != t for _, t in useful)]
    pairs = []
    for s, t in [*useful, *zip(sources, targets, strict=True)]:
        pairs += [(2 * s + core, 2 * t + (core ^ (s == t))) for core in range(2)]
    return pairs


def on_device(propagator, forcing):
    intervals, b, r = forcing.shape
    lines, places = lax.axis_size("rx"), lax.axis_size("ry")
    chips, devices = places // 2, lines * places
    heads = sorted({max(chips // 2 - 1, 0), chips // 2})
    part = r // (2 * len(heads))

    def swap(value):
        return lax.ppermute(value, "ry", [(i, i ^ 1) for i in range(places)])

    def to_heads(value, d):
        return lax.ppermute(value, "ry", filled([(h ^ d, h) for h in heads], chips))

    def from_heads(value, d):
        return lax.ppermute(value, "ry", filled([(h, h ^ d) for h in heads], chips))

    def hops(value, width, first=True):
        out = []
        for j in range(width):
            to = {}
            for block in range(0 if first else 2 * width, 2 * width if first else lines, 2 * width):
                source, target = block + width - 1, block + width + j
                back = target
                to[source], to[target] = target, source
                if back != target:
                    to[target], to[back] = back, source
            if j < width - 1:
                at = [2 * head + core for head in heads for core in range(2)]
                pairs = [(s * places + i, t * places + i) for s, t in to.items() if s < t for i in at]
                out.append(lax.ppermute(value, ("rx", "ry"), pairs))
                continue
            pairs = []
            for g in range(lines):
                for i in range(places):
                    at = to.get(g) if i // 2 in heads else None
                    pairs.append((g * places + i, g * places + (i ^ 1) if at is None else at * places + i))
            out.append(lax.ppermute(value, ("rx", "ry"), pairs))
        return out

    propagator, forcing = (pltpu.with_memory_space_constraint(a, pltpu.HBM) for a in (propagator, forcing))
    own, first, rest = call(
        local_kernel,
        [(b, b + r), (b, b + r), (max(intervals - 1, 1), b, b + r)],
        [pltpu.SemaphoreType.DMA((intervals, 2))],
        spec=HBM,
    )(propagator, forcing)
    other = swap(own)
    soon = [d for d in range(chips) if chips // 2 <= d < max(chips - 1, 1)]
    later = [d for d in range(chips) if d not in soon]
    chip_map, chip_state, *cuts = call(
        functools.partial(chip_kernel, heads, soon), [(b, b), (r, b)] + [(b // 2 + part, b)] * len(soon)
    )(own, other)
    more = call(functools.partial(cut_kernel, heads, later), [(b // 2 + part, b)] * len(later), cost=SHADOW)(
        chip_map, chip_state
    )
    cuts = dict(zip([*soon, *later], [*cuts, *more], strict=True))
    gathered = [to_heads(cuts[d], d) for d in range(1, chips)]
    early, _ = lax.optimization_barrier((first, cuts[0]))
    matrices, constants = call(
        prepare_kernel,
        [halved(intervals, 2, b, b), (intervals, b, r)],
        [pltpu.VMEM((b, b + r), F32)],
        cost=SHADOW,
    )(other, early, rest)
    for d in range(chips - 1):
        gathered[d], _ = lax.optimization_barrier((gathered[d], constants))
    swapped = [swap(value) for value in gathered]
    first_late, _ = lax.optimization_barrier((first, gathered))
    following = lax.ppermute(first_late, ("rx", "ry"), [(i, (i - 1) % devices) for i in range(devices)])
    steps, lineF, line_state = call(
        functools.partial(line_state_kernel, heads, chips),
        [halved(chips, 2, b, b), (chips, part, b), (part, b)],
        [pltpu.VMEM((chips, b, b), F32)],
    )(chip_map, cuts[0], *gathered, *swapped)
    lineP, line_map = call(
        functools.partial(line_map_kernel, heads, chips), [halved(chips, 2, b, b), (b // 2 + part, b)], [pltpu.VMEM((b, b), F32)], cost=SHADOW
    )(steps, line_state)

    total_map, total_state, pre, late = line_map, line_state, [], False
    width, states = 1, []
    while width < lines:
        last = 2 * width >= lines
        if width > 1:
            total_state, *more = call(
                functools.partial(total_kernel, not last), [(part, b)] + [(b // 2 + part, b), (b, b)] * (not last), cost=SHADOW
            )(*pre[: 2 - last], lineP, line_state)
            total_map = more and more[0]
        states = hops(total_state, width)
        if last:
            break
        maps = hops(total_map, width, first=False)
        late = width == 1 and 4 * width >= lines
        if not late:
            maps = [call(whole_kernel, [(b + part, b)])(value, swap(value))[0] for value in maps]
        if width == 1:
            pre = [*states, *maps]
        else:
            pre = call(functools.partial(prefix_kernel, width), [(part, b), (b + part, b)])(*states, *maps, *pre)
        width *= 2
    if late:
        pre[1], _ = lax.optimization_barrier((pre[1], total_state))
        pre += [swap(piece) for piece in call(pieces_kernel, [(b // 4, b)] * 2, cost=1)(pre[1])]
    near, far = range(max(chips // 2, 1)), range(max(chips // 2, 1), chips)
    start, *later = call(
        functools.partial(start_kernel, width, len(states), len(pre), far), [(part, b)] * (1 + len(far)),
        [pltpu.VMEM((b + part, b), F32)],
    )(*states, *pre, lineP, lineF)
    entering = call(functools.partial(enter_kernel, near), [(part, b)] * len(near), cost=SHADOW)(start, lineP, lineF)
    entering = [*entering, *later]
    parts = [entering[0]] + [from_heads(entering[d], d) for d in range(1, chips)]
    following, _ = lax.optimization_barrier((following, start))
    next_matrix, next_constant = call(follow_kernel, [halved(2, b, b), (b, r)], cost=SHADOW)(
        matrices, constants, following
    )
    for d in range(1, chips):
        parts[d], _ = lax.optimization_barrier((parts[d], next_constant))
    shared = {d: swap(parts[d]) for d in range(chips) if d != 1}
    if chips > 1:
        parts[1], shared = lax.optimization_barrier((parts[1], shared))
        shared[1] = swap(parts[1])
    return tuple(
        call(
            functools.partial(run_kernel, heads, chips),
            [(intervals, b, r)] * 2,
            [
                pltpu.VMEM((r, b), F32),
                pltpu.VMEM((intervals, b, r), F32),
                pltpu.VMEM((intervals, b, r), F32),
                pltpu.SemaphoreType.DMA((2, intervals)),
            ],
            out_spec=HBM,
        )(*parts, *[shared[d] for d in range(chips)], matrices, constants, next_matrix, next_constant)
    )


def solution(mesh):
    spec = P(("rx", "ry"), None, None)
    return jax.shard_map(
        on_device, mesh=mesh, in_specs=(spec, spec), out_specs=(spec, spec), check_vma=False
    )
```

```python
import functools

import jax
import jax.numpy as jnp
from jax import lax
from jax.experimental import pallas as pl
from jax.experimental.pallas import tpu as pltpu
from jax.sharding import PartitionSpec as P

F32 = jnp.float32
BF16 = jnp.bfloat16
NN = (((1,), (0,)), ((), ()))
NT = (((1,), (1,)), ((), ()))
VMEM = pl.BlockSpec(memory_space=pltpu.VMEM)
HBM = pl.BlockSpec(memory_space=pltpu.HBM)
SHADOW = 3_000_000_000


def split(value):
    high = value.astype(BF16)
    return high, (value - high.astype(F32)).astype(BF16)


def product(left, right, dims=NN):
    dot = functools.partial(lax.dot_general, dimension_numbers=dims, preferred_element_type=F32)
    return dot(left[0], right[0]) + (dot(left[0], right[1]) + dot(left[1], right[0]))


def call(kernel, outs, scratch=(), spec=VMEM, out_spec=VMEM, cost=0):
    shapes = [out if isinstance(out, jax.ShapeDtypeStruct) else jax.ShapeDtypeStruct(out, F32) for out in outs]

    def run(*args):
        specs = spec if isinstance(spec, list) else [spec] * len(args)
        return pl.pallas_call(
            kernel,
            in_specs=specs,
            out_specs=[out_spec] * len(outs),
            out_shape=shapes,
            scratch_shapes=list(scratch),
            cost_estimate=pl.CostEstimate(flops=cost, bytes_accessed=0, transcendentals=0) if cost else None,
            compiler_params=pltpu.CompilerParams(vmem_limit_bytes=32 * 1024 * 1024),
        )(*args)

    return run


def halved(*shape):
    return jax.ShapeDtypeStruct(shape, BF16)


def put(ref, value, *at):
    ref[*at, 0], ref[*at, 1] = split(value)


def get(ref, *at):
    return ref[*at, 0], ref[*at, 1]


def where():
    place = lax.axis_index("ry")
    return lax.axis_index("rx"), place // 2, place % 2


def rows(start, size):
    return pl.ds(pl.multiple_of(start, 8), size)


def local_kernel(a_ref, f_ref, own_ref, first_ref, rest_ref, sems):
    n, b = a_ref.shape[:2]
    copies = []
    for i in range(n):
        to = first_ref if i == 0 else rest_ref.at[i - 1]
        copies.append(
            (
                pltpu.make_async_copy(a_ref.at[i], to.at[:, pl.ds(0, b)], sems.at[i, 0]),
                pltpu.make_async_copy(f_ref.at[i], to.at[:, pl.ds(b, f_ref.shape[2])], sems.at[i, 1]),
            )
        )
    for part in range(2):
        for i in range(n):
            copies[i][part].start()
    copies[0][0].wait()
    total = first_ref[:, :b]
    steps = []
    for i in range(1, n):
        copies[i][0].wait()
        steps.append(split(rest_ref[i - 1, :, :b]))
        total = product(steps[-1], split(total))
    own_ref[:, :b] = total
    copies[0][1].wait()
    total = first_ref[:, b:]
    for i in range(1, n):
        copies[i][1].wait()
        total = product(steps[i - 1], split(total)) + rest_ref[i - 1, :, b:]
    own_ref[:, b:] = total


def chip_kernel(heads, ds, own_ref, other_ref, map_ref, state_ref, *outs):
    core = where()[2]
    b = own_ref.shape[0]

    def combine(earlier_ref, later_ref):
        later = split(later_ref[:, :b])
        map_ref[...] = product(later, split(earlier_ref[:, :b])).T
        state_ref[...] = (product(later, split(earlier_ref[:, b:])) + later_ref[:, b:]).T

    @pl.when(core == 0)
    def _():
        combine(own_ref, other_ref)

    @pl.when(core == 1)
    def _():
        combine(other_ref, own_ref)

    cut_kernel(heads, ds, map_ref, state_ref, *outs)


def cut_kernel(heads, ds, map_ref, state_ref, *outs):
    _, z, core = where()
    half = map_ref.shape[0] // 2
    part = outs[0].shape[0] - half if outs else 0
    for d, out in zip(ds, outs, strict=True):
        for j, head in enumerate(heads):

            @pl.when(z ^ d == head)
            def _():
                out[:half] = map_ref[rows(core * half, half)]
                out[half:] = state_ref[rows((2 * j + core) * part, part)]


def on_head(heads, body):
    pl.when(functools.reduce(jnp.logical_or, [where()[1] == head for head in heads]))(body)


def line_state_kernel(heads, chips, *refs):
    map_ref, ins, others = refs[0], refs[1 : 1 + chips], refs[1 + chips : 2 * chips]
    steps_ref, pre_ref, total_ref, all_ref = refs[2 * chips :]
    _, z, core = where()
    half = map_ref.shape[0] // 2

    def body():
        all_ref[z] = map_ref[...]
        for d in range(chips):
            pre_ref[z ^ d] = ins[d][half:]
            if d:
                all_ref[z ^ d, rows(core * half, half)] = ins[d][:half]
                all_ref[z ^ d, rows(half - core * half, half)] = others[d - 1][:half]
        total = pre_ref[0]
        for c in range(1, chips):
            here = pre_ref[c]
            pre_ref[c] = total
            put(steps_ref, all_ref[c], c)
            total = product(split(total), get(steps_ref, c)) + here
        total_ref[...] = total
        put(steps_ref, all_ref[0], 0)

    on_head(heads, body)


def line_map_kernel(heads, chips, steps_ref, pre_ref, total_ref, all_ref):
    half = steps_ref.shape[2] // 2

    def body():
        pre_ref[1 % chips] = steps_ref[0]
        total = steps_ref[0, 0].astype(F32) + steps_ref[0, 1].astype(F32)
        for c in range(1, chips):
            total = product(get(pre_ref, c), get(steps_ref, c))
            put(pre_ref, total, (c + 1) % chips)
        all_ref[...] = total
        total_ref[...] = all_ref[rows(where()[2] * half, half)]

    on_head(heads, body)


def total_kernel(whole, *refs):
    pre0_ref, *pre, line_ref, f_ref = refs[: 3 + whole]
    outs = refs[3 + whole :]
    b = line_ref.shape[2]
    step = get(line_ref, 0)
    outs[0][...] = product(split(pre0_ref[...]), step) + f_ref[...]
    if whole:
        half = b // 2
        outs[3][...] = product(split(pre[0][:b]), step)
        outs[1][...] = outs[3][rows(where()[2] * half, half)]
        outs[2][...] = product(split(pre[0][b:]), step) + f_ref[...]


def choose(refs, width, out_ref):
    for j, ref in enumerate(refs):

        @pl.when(where()[0] % width == j)
        def _():
            out_ref[...] = ref[...]


def advance(width, states, pre0, pre, out_ref):
    g = where()[0]

    @pl.when(g // width % 2 == 1)
    def _():
        choose(states, width, out_ref)
        if pre:
            b = out_ref.shape[1]

            @pl.when(g % width != 0)
            def _():
                out_ref[...] = product(split(out_ref[...]), split(pre[0][:b])) + pre[0][b:]

    if pre0:

        @pl.when(g // width % 2 == 0)
        def _():
            out_ref[...] = pre0[0][...]


def pieces_kernel(in_ref, *outs):
    size = outs[0].shape[0]
    for i, out in enumerate(outs):
        out[...] = in_ref[i * size : (i + 1) * size]


def whole_kernel(own_ref, state_ref, *refs):
    others, out_ref = refs[:-1], refs[-1]
    core = where()[2]
    b = out_ref.shape[1]
    half, size = b // 2, b // 2 // len(others)
    out_ref[rows(core * half, half)] = own_ref[...]
    for i, other_ref in enumerate(others):
        out_ref[rows(half - core * half + i * size, size)] = other_ref[...]
    out_ref[b:] = state_ref[...]


def prefix_kernel(width, *refs):
    states, maps, (pre0_ref, pre_ref, out0_ref, out_ref) = refs[:width], refs[width : 2 * width], refs[2 * width :]
    g = where()[0]
    b = pre_ref.shape[1]
    advance(width, states, [pre0_ref], [pre_ref], out0_ref)

    @pl.when(g // width % 2 == 0)
    def _():
        out_ref[...] = pre_ref[...]

    @pl.when(g // width % 2 == 1)
    def _():
        choose(maps, width, out_ref)

        @pl.when(g % width != 0)
        def _():
            out_ref[...] = product(split(out_ref[...]), split(pre_ref[:b]))
            out_ref[b:] += pre_ref[b:]


def start_kernel(width, count, with_pre, ds, *refs):
    states, refs = refs[:count][::-1], refs[count:]
    pre, refs = refs[:with_pre], refs[with_pre:]
    lineP_ref, lineF_ref, start_ref, *outs, pre_ref = refs
    if with_pre > 2:
        whole_kernel(*pre[1:], pre_ref)
    if count:
        advance(width, states, pre[:1], [pre_ref] if with_pre > 2 else pre[1:], start_ref)

    @pl.when(where()[0] == 0)
    def _():
        start_ref[...] = jnp.zeros_like(start_ref)

    enter_kernel(ds, start_ref, lineP_ref, lineF_ref, *outs)


def enter_kernel(ds, start_ref, lineP_ref, lineF_ref, *outs):
    start = split(start_ref[...])
    for d, out in zip(ds, outs, strict=True):
        c = where()[1] ^ d

        @pl.when(c == 0)
        def _():
            out[...] = start_ref[...]

        @pl.when(c != 0)
        def _():
            out[...] = product(start, get(lineP_ref, c)) + lineF_ref[c]


def prepare_kernel(other_ref, first_ref, rest_ref, m_ref, c_ref, now_ref):
    core = where()[2]
    n, b = c_ref.shape[:2]

    @pl.when(core == 0)
    def _():
        now_ref[...] = first_ref[...]

    @pl.when(core == 1)
    def _():
        step = split(first_ref[:, :b])
        now_ref[:, :b] = product(step, split(other_ref[:, :b]))
        now_ref[:, b:] = product(step, split(other_ref[:, b:])) + first_ref[:, b:]

    for i in range(n):
        now = split(now_ref[...])
        m_ref[i, 0], m_ref[i, 1] = now[0][:, :b], now[1][:, :b]
        c_ref[i] = now_ref[:, b:]
        if i < n - 1:
            later = product(split(rest_ref[i, :, :b]), now)
            now_ref[:, :b] = later[:, :b]
            now_ref[:, b:] = later[:, b:] + rest_ref[i, :, b:]


def follow_kernel(m_ref, c_ref, next_ref, out_ref, add_ref):
    n, b = c_ref.shape[:2]
    step = split(next_ref[:, :b])
    put(out_ref, product(step, get(m_ref, n - 1)))
    add_ref[...] = product(step, split(c_ref[n - 1])) + next_ref[:, b:]


def run_kernel(heads, count, *refs):
    parts, shared = refs[:count], refs[count : 2 * count]
    m_ref, c_ref, next_ref, add_ref, x_ref, s_ref, in_ref, xs_ref, ss_ref, sems = refs[2 * count :]
    g, z, core = where()
    n = x_ref.shape[0]
    part = parts[0].shape[0]
    for d in range(count):
        for j, head in enumerate(heads):

            @pl.when(z ^ d == head)
            def _():
                in_ref[rows((2 * j + core) * part, part)] = parts[d][...]
                in_ref[rows((2 * j + 1 - core) * part, part)] = shared[d][...]

    entering = split(in_ref[...])
    copies = [pltpu.make_async_copy(xs_ref.at[i], x_ref.at[i], sems.at[0, i]) for i in range(n)]
    copies += [pltpu.make_async_copy(ss_ref.at[i], s_ref.at[i], sems.at[1, i]) for i in range(n)]
    for i in range(n):
        xs_ref[i] = product(get(m_ref, i), entering, NT) + c_ref[i]
        copies[i].start()
        if i:
            ss_ref[i - 1] = xs_ref[i] - xs_ref[i - 1]
            copies[n + i - 1].start()
    ss_ref[n - 1] = product(get(next_ref), entering, NT) + add_ref[...] - xs_ref[n - 1]

    @pl.when(g * lax.axis_size("ry") + 2 * z + core == lax.axis_size("rx") * lax.axis_size("ry") - 1)
    def _():
        ss_ref[n - 1] = -xs_ref[n - 1]

    copies[2 * n - 1].start()
    for copy in copies:
        copy.wait()


def filled(useful, chips):
    sources = [c for c in range(chips) if all(c != s for s, _ in useful)]
    targets = [c for c in range(chips) if all(c != t for _, t in useful)]
    pairs = []
    for s, t in [*useful, *zip(sources, targets, strict=True)]:
        pairs += [(2 * s + core, 2 * t + (core ^ (s == t))) for core in range(2)]
    return pairs


def on_device(propagator, forcing):
    intervals, b, r = forcing.shape
    lines, places = lax.axis_size("rx"), lax.axis_size("ry")
    chips, devices = places // 2, lines * places
    heads = sorted({max(chips // 2 - 1, 0), chips // 2})
    part = r // (2 * len(heads))

    def swap(value):
        return lax.ppermute(value, "ry", [(i, i ^ 1) for i in range(places)])

    def to_heads(value, d):
        return lax.ppermute(value, "ry", filled([(h ^ d, h) for h in heads], chips))

    def from_heads(value, d):
        return lax.ppermute(value, "ry", filled([(h, h ^ d) for h in heads], chips))

    def hops(value, width, first=True):
        out = []
        for j in range(width):
            to = {(g, i): (g, i ^ 1) for g in range(lines) for i in range(places)}
            for block in range(0 if first else 2 * width, 2 * width if first else lines, 2 * width):
                source, target = block + width - 1, block + width + j
                for head in heads:
                    end = head - 1 if head == heads[0] else head + 1
                    for core in range(2):
                        i, k = 2 * head + core, 2 * end + core
                        to[source, i], to[target, i] = (target, i), (source, i)
            if first and width > 1 and j == width - 1:
                to = {at: there for at, there in to.items() if at[0] == width - 1 and there[0] != at[0]}
            pairs = [(g * places + i, h * places + k) for (g, i), (h, k) in to.items()]
            out.append(lax.ppermute(value, ("rx", "ry"), pairs))
        return out

    propagator, forcing = (pltpu.with_memory_space_constraint(a, pltpu.HBM) for a in (propagator, forcing))
    own, first, rest = call(
        local_kernel,
        [(b, b + r), (b, b + r), (max(intervals - 1, 1), b, b + r)],
        [pltpu.SemaphoreType.DMA((intervals, 2))],
        spec=HBM,
    )(propagator, forcing)
    other = swap(own)
    soon = [d for d in range(chips) if chips // 2 <= d < max(chips - 1, 1)]
    later = [d for d in range(chips) if d not in soon]
    chip_map, chip_state, *cuts = call(
        functools.partial(chip_kernel, heads, soon), [(b, b), (r, b)] + [(b // 2 + part, b)] * len(soon)
    )(own, other)
    more = call(functools.partial(cut_kernel, heads, later), [(b // 2 + part, b)] * len(later), cost=SHADOW)(
        chip_map, chip_state
    )
    cuts = dict(zip([*soon, *later], [*cuts, *more], strict=True))
    gathered = [to_heads(cuts[d], d) for d in range(1, chips)]
    early, _ = lax.optimization_barrier((first, cuts[0]))
    matrices, constants = call(
        prepare_kernel,
        [halved(intervals, 2, b, b), (intervals, b, r)],
        [pltpu.VMEM((b, b + r), F32)],
        cost=SHADOW,
    )(other, early, rest)
    for d in range(chips - 1):
        gathered[d], _ = lax.optimization_barrier((gathered[d], constants))
    swapped = [swap(value) for value in gathered]
    first_late, _ = lax.optimization_barrier((first, gathered))
    following = lax.ppermute(first_late, ("rx", "ry"), [(i, (i - 1) % devices) for i in range(devices)])
    steps, lineF, line_state = call(
        functools.partial(line_state_kernel, heads, chips),
        [halved(chips, 2, b, b), (chips, part, b), (part, b)],
        [pltpu.VMEM((chips, b, b), F32)],
    )(chip_map, cuts[0], *gathered, *swapped)
    lineP, line_map = call(
        functools.partial(line_map_kernel, heads, chips), [halved(chips, 2, b, b), (b // 2, b)], [pltpu.VMEM((b, b), F32)], cost=SHADOW
    )(steps)

    total_map, total_state, other_state, pre, late = line_map, line_state, line_state, [], False
    width, states = 1, []
    while width < lines:
        last = 2 * width >= lines
        if width > 1:
            total_state, *more = call(
                functools.partial(total_kernel, not last), [(part, b)] + [(b // 2, b), (part, b), (b, b)] * (not last), cost=SHADOW
            )(*pre[: 2 - last], lineP, line_state)
            total_map, other_state = more[:2] if more else (None, None)
        states = hops(total_state, width)
        if last:
            break
        halves = hops(total_map, width, first=False)
        maps = hops(other_state, width, first=False)
        late = width == 1 and 4 * width >= lines
        if not late:
            maps = [
                call(whole_kernel, [(b + part, b)])(mine, state, swap(mine))[0]
                for mine, state in zip(halves, maps, strict=True)
            ]
        if width == 1:
            pre = [*states, *maps]
        else:
            pre = call(functools.partial(prefix_kernel, width), [(part, b), (b + part, b)])(*states, *maps, *pre)
        width *= 2
    if late:
        mine, _ = lax.optimization_barrier((halves[0], total_state))
        pieces = call(pieces_kernel, [(b // 4, b)] * 2, cost=1)(mine)
        pre = [pre[0], mine, pre[1], *[swap(piece) for piece in pieces]]
    near, far = range(max(chips // 2, 1)), range(max(chips // 2, 1), chips)
    start, *later = call(
        functools.partial(start_kernel, width, len(states), len(pre), far), [(part, b)] * (1 + len(far)),
        [pltpu.VMEM((b + part, b), F32)],
    )(*states[::-1], *pre, lineP, lineF)
    entering = call(functools.partial(enter_kernel, near), [(part, b)] * len(near), cost=SHADOW)(start, lineP, lineF)
    entering = [*entering, *later]
    parts = [entering[0]] + [from_heads(entering[d], d) for d in range(1, chips)]
    following, _ = lax.optimization_barrier((following, start))
    next_matrix, next_constant = call(follow_kernel, [halved(2, b, b), (b, r)], cost=SHADOW)(
        matrices, constants, following
    )
    for d in range(1, chips):
        parts[d], _ = lax.optimization_barrier((parts[d], next_constant))
    shared = {d: swap(parts[d]) for d in range(chips) if d != 1}
    if chips > 1:
        parts[1], shared = lax.optimization_barrier((parts[1], shared))
        shared[1] = swap(parts[1])
    return tuple(
        call(
            functools.partial(run_kernel, heads, chips),
            [(intervals, b, r)] * 2,
            [
                pltpu.VMEM((r, b), F32),
                pltpu.VMEM((intervals, b, r), F32),
                pltpu.VMEM((intervals, b, r), F32),
                pltpu.SemaphoreType.DMA((2, intervals)),
            ],
            out_spec=HBM,
        )(*parts, *[shared[d] for d in range(chips)], matrices, constants, next_matrix, next_constant)
    )


def solution(mesh):
    spec = P(("rx", "ry"), None, None)
    return jax.shard_map(
        on_device, mesh=mesh, in_specs=(spec, spec), out_specs=(spec, spec), check_vma=False
    )
```

```python
import functools

import jax
import jax.numpy as jnp
from jax import lax
from jax.experimental import pallas as pl
from jax.experimental.pallas import tpu as pltpu
from jax.sharding import PartitionSpec as P

F32 = jnp.float32
BF16 = jnp.bfloat16
NN = (((1,), (0,)), ((), ()))
NT = (((1,), (1,)), ((), ()))
VMEM = pl.BlockSpec(memory_space=pltpu.VMEM)
HBM = pl.BlockSpec(memory_space=pltpu.HBM)
SHADOW = 3_000_000_000


def split(value):
    high = value.astype(BF16)
    return high, (value - high.astype(F32)).astype(BF16)


def product(left, right, dims=NN):
    dot = functools.partial(lax.dot_general, dimension_numbers=dims, preferred_element_type=F32)
    return dot(left[0], right[0]) + (dot(left[0], right[1]) + dot(left[1], right[0]))


def call(kernel, outs, scratch=(), spec=VMEM, out_spec=VMEM, cost=0):
    shapes = [out if isinstance(out, jax.ShapeDtypeStruct) else jax.ShapeDtypeStruct(out, F32) for out in outs]

    def run(*args):
        specs = spec if isinstance(spec, list) else [spec] * len(args)
        return pl.pallas_call(
            kernel,
            in_specs=specs,
            out_specs=[out_spec] * len(outs),
            out_shape=shapes,
            scratch_shapes=list(scratch),
            cost_estimate=pl.CostEstimate(flops=cost, bytes_accessed=0, transcendentals=0) if cost else None,
            compiler_params=pltpu.CompilerParams(vmem_limit_bytes=32 * 1024 * 1024),
        )(*args)

    return run


def halved(*shape):
    return jax.ShapeDtypeStruct(shape, BF16)


def put(ref, value, *at):
    ref[*at, 0], ref[*at, 1] = split(value)


def get(ref, *at):
    return ref[*at, 0], ref[*at, 1]


def where():
    place = lax.axis_index("ry")
    return lax.axis_index("rx"), place // 2, place % 2


def rows(start, size):
    return pl.ds(pl.multiple_of(start, 8), size)


def local_kernel(a_ref, f_ref, own_ref, first_ref, rest_ref, sems):
    n, b = a_ref.shape[:2]
    copies = []
    for i in range(n):
        to = first_ref if i == 0 else rest_ref.at[i - 1]
        copies.append(
            (
                pltpu.make_async_copy(a_ref.at[i], to.at[:, pl.ds(0, b)], sems.at[i, 0]),
                pltpu.make_async_copy(f_ref.at[i], to.at[:, pl.ds(b, f_ref.shape[2])], sems.at[i, 1]),
            )
        )
    for part in range(2):
        for i in range(n):
            copies[i][part].start()
    copies[0][0].wait()
    total = first_ref[:, :b]
    steps = []
    for i in range(1, n):
        copies[i][0].wait()
        steps.append(split(rest_ref[i - 1, :, :b]))
        total = product(steps[-1], split(total))
    own_ref[:, :b] = total
    copies[0][1].wait()
    total = first_ref[:, b:]
    for i in range(1, n):
        copies[i][1].wait()
        total = product(steps[i - 1], split(total)) + rest_ref[i - 1, :, b:]
    own_ref[:, b:] = total


def chip_kernel(heads, ds, own_ref, other_ref, map_ref, state_ref, *outs):
    core = where()[2]
    b = own_ref.shape[0]

    def combine(earlier_ref, later_ref):
        later = split(later_ref[:, :b])
        map_ref[...] = product(later, split(earlier_ref[:, :b])).T
        state_ref[...] = (product(later, split(earlier_ref[:, b:])) + later_ref[:, b:]).T

    @pl.when(core == 0)
    def _():
        combine(own_ref, other_ref)

    @pl.when(core == 1)
    def _():
        combine(other_ref, own_ref)

    cut_kernel(heads, ds, map_ref, state_ref, *outs)


def cut_kernel(heads, ds, map_ref, state_ref, *outs):
    _, z, core = where()
    half = map_ref.shape[0] // 2
    part = outs[0].shape[0] - half if outs else 0
    for d, out in zip(ds, outs, strict=True):
        for j, head in enumerate(heads):

            @pl.when(z ^ d == head)
            def _():
                out[:half] = map_ref[rows(core * half, half)]
                out[half:] = state_ref[rows((2 * j + core) * part, part)]


def on_head(heads, body):
    pl.when(functools.reduce(jnp.logical_or, [where()[1] == head for head in heads]))(body)


def line_state_kernel(heads, chips, *refs):
    map_ref, ins, others = refs[0], refs[1 : 1 + chips], refs[1 + chips : 2 * chips]
    steps_ref, pre_ref, total_ref, all_ref = refs[2 * chips :]
    _, z, core = where()
    half = map_ref.shape[0] // 2

    def body():
        all_ref[z] = map_ref[...]
        for d in range(chips):
            pre_ref[z ^ d] = ins[d][half:]
            if d:
                all_ref[z ^ d, rows(core * half, half)] = ins[d][:half]
                all_ref[z ^ d, rows(half - core * half, half)] = others[d - 1][:half]
        total = pre_ref[0]
        for c in range(1, chips):
            here = pre_ref[c]
            pre_ref[c] = total
            put(steps_ref, all_ref[c], c)
            total = product(split(total), get(steps_ref, c)) + here
        total_ref[...] = total
        put(steps_ref, all_ref[0], 0)

    on_head(heads, body)


def line_map_kernel(heads, chips, steps_ref, pre_ref, total_ref, all_ref):
    half = steps_ref.shape[2] // 2

    def body():
        pre_ref[1 % chips] = steps_ref[0]
        total = steps_ref[0, 0].astype(F32) + steps_ref[0, 1].astype(F32)
        for c in range(1, chips):
            total = product(get(pre_ref, c), get(steps_ref, c))
            put(pre_ref, total, (c + 1) % chips)
        all_ref[...] = total
        total_ref[...] = all_ref[rows(where()[2] * half, half)]

    on_head(heads, body)


def total_kernel(whole, *refs):
    pre0_ref, *pre, line_ref, f_ref = refs[: 3 + whole]
    outs = refs[3 + whole :]
    b = line_ref.shape[2]
    step = get(line_ref, 0)
    outs[0][...] = product(split(pre0_ref[...]), step) + f_ref[...]
    if whole:
        half = b // 2
        outs[3][...] = product(split(pre[0][:b]), step)
        outs[1][...] = outs[3][rows(where()[2] * half, half)]
        outs[2][...] = product(split(pre[0][b:]), step) + f_ref[...]


def choose(refs, width, out_ref):
    for j, ref in enumerate(refs):

        @pl.when(where()[0] % width == j)
        def _():
            out_ref[...] = ref[...]


def advance(width, states, pre0, pre, out_ref):
    g = where()[0]

    @pl.when(g // width % 2 == 1)
    def _():
        choose(states, width, out_ref)
        if pre:
            b = out_ref.shape[1]

            @pl.when(g % width != 0)
            def _():
                out_ref[...] = product(split(out_ref[...]), split(pre[0][:b])) + pre[0][b:]

    if pre0:

        @pl.when(g // width % 2 == 0)
        def _():
            out_ref[...] = pre0[0][...]


def pieces_kernel(in_ref, *outs):
    size = outs[0].shape[0]
    for i, out in enumerate(outs):
        out[...] = in_ref[i * size : (i + 1) * size]


def whole_kernel(own_ref, state_ref, *refs):
    others, out_ref = refs[:-1], refs[-1]
    core = where()[2]
    b = out_ref.shape[1]
    half, size = b // 2, b // 2 // len(others)
    out_ref[rows(core * half, half)] = own_ref[...]
    for i, other_ref in enumerate(others):
        out_ref[rows(half - core * half + i * size, size)] = other_ref[...]
    out_ref[b:] = state_ref[...]


def prefix_kernel(width, *refs):
    states, maps, (pre0_ref, pre_ref, out0_ref, out_ref) = refs[:width], refs[width : 2 * width], refs[2 * width :]
    g = where()[0]
    b = pre_ref.shape[1]
    advance(width, states, [pre0_ref], [pre_ref], out0_ref)

    @pl.when(g // width % 2 == 0)
    def _():
        out_ref[...] = pre_ref[...]

    @pl.when(g // width % 2 == 1)
    def _():
        choose(maps, width, out_ref)

        @pl.when(g % width != 0)
        def _():
            out_ref[...] = product(split(out_ref[...]), split(pre_ref[:b]))
            out_ref[b:] += pre_ref[b:]


def start_kernel(width, count, with_pre, ds, *refs):
    states, refs = refs[:count][::-1], refs[count:]
    pre, refs = refs[:with_pre], refs[with_pre:]
    lineP_ref, lineF_ref, start_ref, *outs, pre_ref = refs
    if with_pre > 2:
        whole_kernel(*pre[1:], pre_ref)
    if count:
        advance(width, states, pre[:1], [pre_ref] if with_pre > 2 else pre[1:], start_ref)

    @pl.when(where()[0] == 0)
    def _():
        start_ref[...] = jnp.zeros_like(start_ref)

    enter_kernel(ds, start_ref, lineP_ref, lineF_ref, *outs)


def enter_kernel(ds, start_ref, lineP_ref, lineF_ref, *outs):
    start = split(start_ref[...])
    for d, out in zip(ds, outs, strict=True):
        c = where()[1] ^ d

        @pl.when(c == 0)
        def _():
            out[...] = start_ref[...]

        @pl.when(c != 0)
        def _():
            out[...] = product(start, get(lineP_ref, c)) + lineF_ref[c]


def prepare_kernel(other_ref, first_ref, rest_ref, m_ref, c_ref, now_ref):
    core = where()[2]
    n, b = c_ref.shape[:2]

    @pl.when(core == 0)
    def _():
        now_ref[...] = first_ref[...]

    @pl.when(core == 1)
    def _():
        step = split(first_ref[:, :b])
        now_ref[:, :b] = product(step, split(other_ref[:, :b]))
        now_ref[:, b:] = product(step, split(other_ref[:, b:])) + first_ref[:, b:]

    for i in range(n):
        now = split(now_ref[...])
        m_ref[i, 0], m_ref[i, 1] = now[0][:, :b], now[1][:, :b]
        c_ref[i] = now_ref[:, b:]
        if i < n - 1:
            later = product(split(rest_ref[i, :, :b]), now)
            now_ref[:, :b] = later[:, :b]
            now_ref[:, b:] = later[:, b:] + rest_ref[i, :, b:]


def follow_kernel(m_ref, c_ref, next_ref, out_ref, add_ref):
    n, b = c_ref.shape[:2]
    step = split(next_ref[:, :b])
    put(out_ref, product(step, get(m_ref, n - 1)))
    add_ref[...] = product(step, split(c_ref[n - 1])) + next_ref[:, b:]


def run_kernel(heads, count, *refs):
    parts, shared = refs[:count], refs[count : 2 * count]
    m_ref, c_ref, next_ref, add_ref, x_ref, s_ref, in_ref, xs_ref, ss_ref, sems = refs[2 * count :]
    g, z, core = where()
    n = x_ref.shape[0]
    part = parts[0].shape[0]
    for d in range(count):
        for j, head in enumerate(heads):

            @pl.when(z ^ d == head)
            def _():
                in_ref[rows((2 * j + core) * part, part)] = parts[d][...]
                in_ref[rows((2 * j + 1 - core) * part, part)] = shared[d][...]

    entering = split(in_ref[...])
    copies = [pltpu.make_async_copy(xs_ref.at[i], x_ref.at[i], sems.at[0, i]) for i in range(n)]
    copies += [pltpu.make_async_copy(ss_ref.at[i], s_ref.at[i], sems.at[1, i]) for i in range(n - 1)]
    for i in range(n):
        xs_ref[i] = product(get(m_ref, i), entering, NT) + c_ref[i]
        copies[i].start()
        if i:
            ss_ref[i - 1] = xs_ref[i] - xs_ref[i - 1]
            copies[n + i - 1].start()
    last = g * lax.axis_size("ry") + 2 * z + core == lax.axis_size("rx") * lax.axis_size("ry") - 1
    half = xs_ref.shape[1] // 2
    ends = []
    for k in range(2):
        at = slice(k * half, (k + 1) * half)
        following = product((next_ref[0, at], next_ref[1, at]), entering, NT) + add_ref[at]
        ss_ref[n - 1, at] = jnp.where(last, 0.0, following) - xs_ref[n - 1, at]
        span = pl.ds(k * half, half)
        ends.append(pltpu.make_async_copy(ss_ref.at[n - 1, span], s_ref.at[n - 1, span], sems.at[1, n - 1 + k]))
        ends[-1].start()
    for copy in [*copies[: 2 * n - 1], *ends]:
        copy.wait()


def filled(useful, chips):
    sources = [c for c in range(chips) if all(c != s for s, _ in useful)]
    targets = [c for c in range(chips) if all(c != t for _, t in useful)]
    pairs = []
    for s, t in [*useful, *zip(sources, targets, strict=True)]:
        pairs += [(2 * s + core, 2 * t + (core ^ (s == t))) for core in range(2)]
    return pairs


def on_device(propagator, forcing):
    intervals, b, r = forcing.shape
    lines, places = lax.axis_size("rx"), lax.axis_size("ry")
    chips, devices = places // 2, lines * places
    heads = sorted({max(chips // 2 - 1, 0), chips // 2})
    part = r // (2 * len(heads))

    def swap(value):
        return lax.ppermute(value, "ry", [(i, i ^ 1) for i in range(places)])

    def to_heads(value, d):
        return lax.ppermute(value, "ry", filled([(h ^ d, h) for h in heads], chips))

    def from_heads(value, d):
        return lax.ppermute(value, "ry", filled([(h, h ^ d) for h in heads], chips))

    def hops(value, width, first=True):
        out = []
        for j in range(width):
            to = {(g, i): (g, i ^ 1) for g in range(lines) for i in range(places)}
            for block in range(0 if first else 2 * width, 2 * width if first else lines, 2 * width):
                source, target = block + width - 1, block + width + j
                for head in heads:
                    end = head - 1 if head == heads[0] else head + 1
                    for core in range(2):
                        i, k = 2 * head + core, 2 * end + core
                        to[source, i], to[target, i] = (target, i), (source, i)
            if first and width > 1 and j == width - 1:
                to = {at: there for at, there in to.items() if at[0] == width - 1 and there[0] != at[0]}
            pairs = [(g * places + i, h * places + k) for (g, i), (h, k) in to.items()]
            out.append(lax.ppermute(value, ("rx", "ry"), pairs))
        return out

    propagator, forcing = (pltpu.with_memory_space_constraint(a, pltpu.HBM) for a in (propagator, forcing))
    own, first, rest = call(
        local_kernel,
        [(b, b + r), (b, b + r), (max(intervals - 1, 1), b, b + r)],
        [pltpu.SemaphoreType.DMA((intervals, 2))],
        spec=HBM,
    )(propagator, forcing)
    other = swap(own)
    soon = [d for d in range(chips) if chips // 2 <= d < max(chips - 1, 1)]
    later = [d for d in range(chips) if d not in soon]
    chip_map, chip_state, *cuts = call(
        functools.partial(chip_kernel, heads, soon), [(b, b), (r, b)] + [(b // 2 + part, b)] * len(soon)
    )(own, other)
    more = call(functools.partial(cut_kernel, heads, later), [(b // 2 + part, b)] * len(later), cost=SHADOW)(
        chip_map, chip_state
    )
    cuts = dict(zip([*soon, *later], [*cuts, *more], strict=True))
    gathered = [to_heads(cuts[d], d) for d in range(1, chips)]
    early, _ = lax.optimization_barrier((first, cuts[0]))
    matrices, constants = call(
        prepare_kernel,
        [halved(intervals, 2, b, b), (intervals, b, r)],
        [pltpu.VMEM((b, b + r), F32)],
        cost=SHADOW,
    )(other, early, rest)
    for d in range(chips - 1):
        gathered[d], _ = lax.optimization_barrier((gathered[d], constants))
    swapped = [swap(value) for value in gathered]
    first_late, _ = lax.optimization_barrier((first, gathered))
    following = lax.ppermute(first_late, ("rx", "ry"), [(i, (i - 1) % devices) for i in range(devices)])
    steps, lineF, line_state = call(
        functools.partial(line_state_kernel, heads, chips),
        [halved(chips, 2, b, b), (chips, part, b), (part, b)],
        [pltpu.VMEM((chips, b, b), F32)],
    )(chip_map, cuts[0], *gathered, *swapped)
    lineP, line_map = call(
        functools.partial(line_map_kernel, heads, chips), [halved(chips, 2, b, b), (b // 2, b)], [pltpu.VMEM((b, b), F32)], cost=SHADOW
    )(steps)

    total_map, total_state, other_state, pre, late = line_map, line_state, line_state, [], False
    width, states = 1, []
    while width < lines:
        last = 2 * width >= lines
        if width > 1:
            total_state, *more = call(
                functools.partial(total_kernel, not last), [(part, b)] + [(b // 2, b), (part, b), (b, b)] * (not last), cost=SHADOW
            )(*pre[: 2 - last], lineP, line_state)
            total_map, other_state = more[:2] if more else (None, None)
        states = hops(total_state, width)
        if last:
            break
        halves = hops(total_map, width, first=False)
        maps = hops(other_state, width, first=False)
        late = width == 1 and 4 * width >= lines
        if not late:
            maps = [
                call(whole_kernel, [(b + part, b)])(mine, state, swap(mine))[0]
                for mine, state in zip(halves, maps, strict=True)
            ]
        if width == 1:
            pre = [*states, *maps]
        else:
            pre = call(functools.partial(prefix_kernel, width), [(part, b), (b + part, b)])(*states, *maps, *pre)
        width *= 2
    if late:
        mine, _ = lax.optimization_barrier((halves[0], total_state))
        pieces = call(pieces_kernel, [(b // 4, b)] * 2, cost=1)(mine)
        pre = [pre[0], mine, pre[1], *[swap(piece) for piece in pieces]]
    near, far = range(max(chips // 2, 1)), range(max(chips // 2, 1), chips)
    start, *later = call(
        functools.partial(start_kernel, width, len(states), len(pre), far), [(part, b)] * (1 + len(far)),
        [pltpu.VMEM((b + part, b), F32)],
    )(*states[::-1], *pre, lineP, lineF)
    entering = call(functools.partial(enter_kernel, near), [(part, b)] * len(near), cost=SHADOW)(start, lineP, lineF)
    entering = [*entering, *later]
    parts = [entering[0]] + [from_heads(entering[d], d) for d in range(1, chips)]
    following, _ = lax.optimization_barrier((following, start))
    next_matrix, next_constant = call(follow_kernel, [halved(2, b, b), (b, r)], cost=SHADOW)(
        matrices, constants, following
    )
    for d in range(1, chips):
        parts[d], _ = lax.optimization_barrier((parts[d], next_constant))
    shared = {d: swap(parts[d]) for d in range(chips) if d != 1}
    if chips > 1:
        parts[1], shared = lax.optimization_barrier((parts[1], shared))
        shared[1] = swap(parts[1])
    return tuple(
        call(
            functools.partial(run_kernel, heads, chips),
            [(intervals, b, r)] * 2,
            [
                pltpu.VMEM((r, b), F32),
                pltpu.VMEM((intervals, b, r), F32),
                pltpu.VMEM((intervals, b, r), F32),
                pltpu.SemaphoreType.DMA((2, intervals + 1)),
            ],
            out_spec=HBM,
        )(*parts, *[shared[d] for d in range(chips)], matrices, constants, next_matrix, next_constant)
    )


def solution(mesh):
    spec = P(("rx", "ry"), None, None)
    return jax.shard_map(
        on_device, mesh=mesh, in_specs=(spec, spec), out_specs=(spec, spec), check_vma=False
    )
```

```python
import functools

import jax
import jax.numpy as jnp
from jax import lax
from jax.experimental import pallas as pl
from jax.experimental.pallas import tpu as pltpu
from jax.sharding import PartitionSpec as P

F32 = jnp.float32
BF16 = jnp.bfloat16
NN = (((1,), (0,)), ((), ()))
NT = (((1,), (1,)), ((), ()))
VMEM = pl.BlockSpec(memory_space=pltpu.VMEM)
HBM = pl.BlockSpec(memory_space=pltpu.HBM)
SHADOW = 3_000_000_000


def split(value):
    high = value.astype(BF16)
    return high, (value - high.astype(F32)).astype(BF16)


def product(left, right, dims=NN):
    dot = functools.partial(lax.dot_general, dimension_numbers=dims, preferred_element_type=F32)
    return dot(left[0], right[0]) + (dot(left[0], right[1]) + dot(left[1], right[0]))


def call(kernel, outs, scratch=(), spec=VMEM, out_spec=VMEM, cost=0):
    shapes = [out if isinstance(out, jax.ShapeDtypeStruct) else jax.ShapeDtypeStruct(out, F32) for out in outs]

    def run(*args):
        specs = spec if isinstance(spec, list) else [spec] * len(args)
        return pl.pallas_call(
            kernel,
            in_specs=specs,
            out_specs=[out_spec] * len(outs),
            out_shape=shapes,
            scratch_shapes=list(scratch),
            cost_estimate=pl.CostEstimate(flops=cost, bytes_accessed=0, transcendentals=0) if cost else None,
            compiler_params=pltpu.CompilerParams(vmem_limit_bytes=32 * 1024 * 1024),
        )(*args)

    return run


def halved(*shape):
    return jax.ShapeDtypeStruct(shape, BF16)


def put(ref, value, *at):
    ref[*at, 0], ref[*at, 1] = split(value)


def get(ref, *at):
    return ref[*at, 0], ref[*at, 1]


def where():
    place = lax.axis_index("ry")
    return lax.axis_index("rx"), place // 2, place % 2


def rows(start, size):
    return pl.ds(pl.multiple_of(start, 8), size)


def local_kernel(a_ref, f_ref, own_ref, first_ref, rest_ref, sems):
    n, b = a_ref.shape[:2]
    copies = []
    for i in range(n):
        to = first_ref if i == 0 else rest_ref.at[i - 1]
        copies.append(
            (
                pltpu.make_async_copy(a_ref.at[i], to.at[:, pl.ds(0, b)], sems.at[i, 0]),
                pltpu.make_async_copy(f_ref.at[i], to.at[:, pl.ds(b, f_ref.shape[2])], sems.at[i, 1]),
            )
        )
    for part in range(2):
        for i in range(n):
            copies[i][part].start()
    copies[0][0].wait()
    total = first_ref[:, :b]
    steps = []
    for i in range(1, n):
        copies[i][0].wait()
        steps.append(split(rest_ref[i - 1, :, :b]))
        total = product(steps[-1], split(total))
    own_ref[:, :b] = total
    copies[0][1].wait()
    total = first_ref[:, b:]
    for i in range(1, n):
        copies[i][1].wait()
        total = product(steps[i - 1], split(total)) + rest_ref[i - 1, :, b:]
    own_ref[:, b:] = total


def chip_kernel(heads, ds, own_ref, other_ref, map_ref, state_ref, *outs):
    core = where()[2]
    b = own_ref.shape[0]

    def combine(earlier_ref, later_ref):
        later = split(later_ref[:, :b])
        map_ref[...] = product(later, split(earlier_ref[:, :b])).T
        state_ref[...] = (product(later, split(earlier_ref[:, b:])) + later_ref[:, b:]).T

    @pl.when(core == 0)
    def _():
        combine(own_ref, other_ref)

    @pl.when(core == 1)
    def _():
        combine(other_ref, own_ref)

    cut_kernel(heads, ds, map_ref, state_ref, *outs)


def cut_kernel(heads, ds, map_ref, state_ref, *outs):
    _, z, core = where()
    half = map_ref.shape[0] // 2
    part = outs[0].shape[0] - half if outs else 0
    for d, out in zip(ds, outs, strict=True):
        for j, head in enumerate(heads):

            @pl.when(z ^ d == head)
            def _():
                out[:half] = map_ref[rows(core * half, half)]
                out[half:] = state_ref[rows((2 * j + core) * part, part)]


def on_head(heads, body):
    pl.when(functools.reduce(jnp.logical_or, [where()[1] == head for head in heads]))(body)


def line_state_kernel(heads, chips, *refs):
    map_ref, ins, others = refs[0], refs[1 : 1 + chips], refs[1 + chips : 2 * chips]
    steps_ref, pre_ref, total_ref, all_ref = refs[2 * chips :]
    _, z, core = where()
    half = map_ref.shape[0] // 2

    def body():
        all_ref[z] = map_ref[...]
        for d in range(chips):
            pre_ref[z ^ d] = ins[d][half:]
            if d:
                all_ref[z ^ d, rows(core * half, half)] = ins[d][:half]
                all_ref[z ^ d, rows(half - core * half, half)] = others[d - 1][:half]
        total = pre_ref[0]
        for c in range(1, chips):
            here = pre_ref[c]
            pre_ref[c] = total
            put(steps_ref, all_ref[c], c)
            total = product(split(total), get(steps_ref, c)) + here
        total_ref[...] = total
        put(steps_ref, all_ref[0], 0)

    on_head(heads, body)


def line_map_kernel(heads, chips, steps_ref, pre_ref, total_ref, all_ref):
    half = steps_ref.shape[2] // 2

    def body():
        pre_ref[1 % chips] = steps_ref[0]
        total = steps_ref[0, 0].astype(F32) + steps_ref[0, 1].astype(F32)
        for c in range(1, chips):
            total = product(get(pre_ref, c), get(steps_ref, c))
            put(pre_ref, total, (c + 1) % chips)
        all_ref[...] = total
        total_ref[...] = all_ref[rows(where()[2] * half, half)]

    on_head(heads, body)


def total_kernel(whole, *refs):
    pre0_ref, *pre, line_ref, f_ref = refs[: 3 + whole]
    outs = refs[3 + whole :]
    b = line_ref.shape[2]
    step = get(line_ref, 0)
    outs[0][...] = product(split(pre0_ref[...]), step) + f_ref[...]
    if whole:
        half = b // 2
        outs[3][...] = product(split(pre[0][:b]), step)
        outs[1][...] = outs[3][rows(where()[2] * half, half)]
        outs[2][...] = product(split(pre[0][b:]), step) + f_ref[...]


def choose(refs, width, out_ref):
    for j, ref in enumerate(refs):

        @pl.when(where()[0] % width == j)
        def _():
            out_ref[...] = ref[...]


def advance(width, states, pre0, pre, out_ref):
    g = where()[0]

    @pl.when(g // width % 2 == 1)
    def _():
        choose(states, width, out_ref)
        if pre:
            b = out_ref.shape[1]

            @pl.when(g % width != 0)
            def _():
                out_ref[...] = product(split(out_ref[...]), split(pre[0][:b])) + pre[0][b:]

    if pre0:

        @pl.when(g // width % 2 == 0)
        def _():
            out_ref[...] = pre0[0][...]


def pieces_kernel(in_ref, *outs):
    size = outs[0].shape[0]
    for i, out in enumerate(outs):
        out[...] = in_ref[i * size : (i + 1) * size]


def whole_kernel(own_ref, state_ref, *refs):
    others, out_ref = refs[:-1], refs[-1]
    core = where()[2]
    b = out_ref.shape[1]
    half, size = b // 2, b // 2 // len(others)
    out_ref[rows(core * half, half)] = own_ref[...]
    for i, other_ref in enumerate(others):
        out_ref[rows(half - core * half + i * size, size)] = other_ref[...]
    out_ref[b:] = state_ref[...]


def prefix_kernel(width, *refs):
    states, maps, (pre0_ref, pre_ref, out0_ref, out_ref) = refs[:width], refs[width : 2 * width], refs[2 * width :]
    g = where()[0]
    b = pre_ref.shape[1]
    advance(width, states, [pre0_ref], [pre_ref], out0_ref)

    @pl.when(g // width % 2 == 0)
    def _():
        out_ref[...] = pre_ref[...]

    @pl.when(g // width % 2 == 1)
    def _():
        choose(maps, width, out_ref)

        @pl.when(g % width != 0)
        def _():
            out_ref[...] = product(split(out_ref[...]), split(pre_ref[:b]))
            out_ref[b:] += pre_ref[b:]


def start_kernel(width, count, with_pre, ds, *refs):
    states, refs = refs[:count][::-1], refs[count:]
    pre, refs = refs[:with_pre], refs[with_pre:]
    lineP_ref, lineF_ref, start_ref, *outs, pre_ref = refs
    if with_pre > 2:
        g = where()[0]

        @pl.when((g // width % 2 == 1) & (g % width != 0))
        def _():
            whole_kernel(*pre[1:], pre_ref)

    if count:
        advance(width, states, pre[:1], [pre_ref] if with_pre > 2 else pre[1:], start_ref)

    @pl.when(where()[0] == 0)
    def _():
        start_ref[...] = jnp.zeros_like(start_ref)

    enter_kernel(ds, start_ref, lineP_ref, lineF_ref, *outs)


def enter_kernel(ds, start_ref, lineP_ref, lineF_ref, *outs):
    start = split(start_ref[...])
    for d, out in zip(ds, outs, strict=True):
        c = where()[1] ^ d

        @pl.when(c == 0)
        def _():
            out[...] = start_ref[...]

        @pl.when(c != 0)
        def _():
            out[...] = product(start, get(lineP_ref, c)) + lineF_ref[c]


def prepare_kernel(other_ref, first_ref, rest_ref, m_ref, c_ref, now_ref):
    core = where()[2]
    n, b = c_ref.shape[:2]

    @pl.when(core == 0)
    def _():
        now_ref[...] = first_ref[...]

    @pl.when(core == 1)
    def _():
        step = split(first_ref[:, :b])
        now_ref[:, :b] = product(step, split(other_ref[:, :b]))
        now_ref[:, b:] = product(step, split(other_ref[:, b:])) + first_ref[:, b:]

    for i in range(n):
        now = split(now_ref[...])
        m_ref[i, 0], m_ref[i, 1] = now[0][:, :b], now[1][:, :b]
        c_ref[i] = now_ref[:, b:]
        if i < n - 1:
            later = product(split(rest_ref[i, :, :b]), now)
            now_ref[:, :b] = later[:, :b]
            now_ref[:, b:] = later[:, b:] + rest_ref[i, :, b:]


def follow_kernel(m_ref, c_ref, next_ref, out_ref, add_ref):
    n, b = c_ref.shape[:2]
    step = split(next_ref[:, :b])
    put(out_ref, product(step, get(m_ref, n - 1)))
    add_ref[...] = product(step, split(c_ref[n - 1])) + next_ref[:, b:]


def run_kernel(heads, count, *refs):
    parts, shared = refs[:count], refs[count : 2 * count]
    m_ref, c_ref, next_ref, add_ref, x_ref, s_ref, in_ref, xs_ref, ss_ref, sems = refs[2 * count :]
    g, z, core = where()
    n = x_ref.shape[0]
    part = parts[0].shape[0]
    for d in range(count):
        for j, head in enumerate(heads):

            @pl.when(z ^ d == head)
            def _():
                in_ref[rows((2 * j + core) * part, part)] = parts[d][...]
                in_ref[rows((2 * j + 1 - core) * part, part)] = shared[d][...]

    entering = split(in_ref[...])
    copies = [pltpu.make_async_copy(xs_ref.at[i], x_ref.at[i], sems.at[0, i]) for i in range(n)]
    copies += [pltpu.make_async_copy(ss_ref.at[i], s_ref.at[i], sems.at[1, i]) for i in range(n)]
    for i in range(n):
        xs_ref[i] = product(get(m_ref, i), entering, NT) + c_ref[i]
        copies[i].start()
        if i:
            ss_ref[i - 1] = xs_ref[i] - xs_ref[i - 1]
            copies[n + i - 1].start()
    ss_ref[n - 1] = product(get(next_ref), entering, NT) + add_ref[...] - xs_ref[n - 1]

    @pl.when(g * lax.axis_size("ry") + 2 * z + core == lax.axis_size("rx") * lax.axis_size("ry") - 1)
    def _():
        ss_ref[n - 1] = -xs_ref[n - 1]

    copies[2 * n - 1].start()
    for copy in copies:
        copy.wait()


def filled(useful, chips):
    sources = [c for c in range(chips) if all(c != s for s, _ in useful)]
    targets = [c for c in range(chips) if all(c != t for _, t in useful)]
    pairs = []
    for s, t in [*useful, *zip(sources, targets, strict=True)]:
        pairs += [(2 * s + core, 2 * t + (core ^ (s == t))) for core in range(2)]
    return pairs


def on_device(propagator, forcing):
    intervals, b, r = forcing.shape
    lines, places = lax.axis_size("rx"), lax.axis_size("ry")
    chips, devices = places // 2, lines * places
    heads = sorted({max(chips // 2 - 1, 0), chips // 2})
    part = r // (2 * len(heads))

    def swap(value):
        return lax.ppermute(value, "ry", [(i, i ^ 1) for i in range(places)])

    def to_heads(value, d):
        return lax.ppermute(value, "ry", filled([(h ^ d, h) for h in heads], chips))

    def from_heads(value, d):
        return lax.ppermute(value, "ry", filled([(h, h ^ d) for h in heads], chips))

    def hops(value, width, first=True):
        out = []
        for j in range(width):
            to = {(g, i): (g, i ^ 1) for g in range(lines) for i in range(places)}
            for block in range(0 if first else 2 * width, 2 * width if first else lines, 2 * width):
                source, target = block + width - 1, block + width + j
                for head in heads:
                    end = head - 1 if head == heads[0] else head + 1
                    for core in range(2):
                        i, k = 2 * head + core, 2 * end + core
                        to[source, i], to[target, i] = (target, i), (source, i)
            if first and width > 1 and j == width - 1:
                to = {at: there for at, there in to.items() if at[0] == width - 1 and there[0] != at[0]}
            pairs = [(g * places + i, h * places + k) for (g, i), (h, k) in to.items()]
            out.append(lax.ppermute(value, ("rx", "ry"), pairs))
        return out

    propagator, forcing = (pltpu.with_memory_space_constraint(a, pltpu.HBM) for a in (propagator, forcing))
    own, first, rest = call(
        local_kernel,
        [(b, b + r), (b, b + r), (max(intervals - 1, 1), b, b + r)],
        [pltpu.SemaphoreType.DMA((intervals, 2))],
        spec=HBM,
    )(propagator, forcing)
    other = swap(own)
    soon = [d for d in range(chips) if chips // 2 <= d < max(chips - 1, 1)]
    later = [d for d in range(chips) if d not in soon]
    chip_map, chip_state, *cuts = call(
        functools.partial(chip_kernel, heads, soon), [(b, b), (r, b)] + [(b // 2 + part, b)] * len(soon)
    )(own, other)
    more = call(functools.partial(cut_kernel, heads, later), [(b // 2 + part, b)] * len(later), cost=SHADOW)(
        chip_map, chip_state
    )
    cuts = dict(zip([*soon, *later], [*cuts, *more], strict=True))
    gathered = [to_heads(cuts[d], d) for d in range(1, chips)]
    early, _ = lax.optimization_barrier((first, cuts[0]))
    matrices, constants = call(
        prepare_kernel,
        [halved(intervals, 2, b, b), (intervals, b, r)],
        [pltpu.VMEM((b, b + r), F32)],
        cost=SHADOW,
    )(other, early, rest)
    for d in range(chips - 1):
        gathered[d], _ = lax.optimization_barrier((gathered[d], constants))
    swapped = [swap(value) for value in gathered]
    first_late, _ = lax.optimization_barrier((first, gathered))
    following = lax.ppermute(first_late, ("rx", "ry"), [(i, (i - 1) % devices) for i in range(devices)])
    steps, lineF, line_state = call(
        functools.partial(line_state_kernel, heads, chips),
        [halved(chips, 2, b, b), (chips, part, b), (part, b)],
        [pltpu.VMEM((chips, b, b), F32)],
    )(chip_map, cuts[0], *gathered, *swapped)
    lineP, line_map = call(
        functools.partial(line_map_kernel, heads, chips), [halved(chips, 2, b, b), (b // 2, b)], [pltpu.VMEM((b, b), F32)], cost=SHADOW
    )(steps)

    total_map, total_state, other_state, pre, late = line_map, line_state, line_state, [], False
    width, states = 1, []
    while width < lines:
        last = 2 * width >= lines
        if width > 1:
            total_state, *more = call(
                functools.partial(total_kernel, not last), [(part, b)] + [(b // 2, b), (part, b), (b, b)] * (not last), cost=SHADOW
            )(*pre[: 2 - last], lineP, line_state)
            total_map, other_state = more[:2] if more else (None, None)
        states = hops(total_state, width)
        if last:
            break
        halves = hops(total_map, width, first=False)
        maps = hops(other_state, width, first=False)
        late = width == 1 and 4 * width >= lines
        if not late:
            maps = [
                call(whole_kernel, [(b + part, b)])(mine, state, swap(mine))[0]
                for mine, state in zip(halves, maps, strict=True)
            ]
        if width == 1:
            pre = [*states, *maps]
        else:
            pre = call(functools.partial(prefix_kernel, width), [(part, b), (b + part, b)])(*states, *maps, *pre)
        width *= 2
    if late:
        mine, _ = lax.optimization_barrier((halves[0], total_state))
        pieces = call(pieces_kernel, [(b // 4, b)] * 2, cost=1)(mine)
        pre = [pre[0], mine, pre[1], *[swap(piece) for piece in pieces]]
    near, far = range(max(chips // 2, 1)), range(max(chips // 2, 1), chips)
    start, *later = call(
        functools.partial(start_kernel, width, len(states), len(pre), far), [(part, b)] * (1 + len(far)),
        [pltpu.VMEM((b + part, b), F32)],
    )(*states[::-1], *pre, lineP, lineF)
    entering = call(functools.partial(enter_kernel, near), [(part, b)] * len(near), cost=SHADOW)(start, lineP, lineF)
    entering = [*entering, *later]
    parts = [entering[0]] + [from_heads(entering[d], d) for d in range(1, chips)]
    following, _ = lax.optimization_barrier((following, start))
    next_matrix, next_constant = call(follow_kernel, [halved(2, b, b), (b, r)], cost=SHADOW)(
        matrices, constants, following
    )
    for d in range(1, chips):
        parts[d], _ = lax.optimization_barrier((parts[d], next_constant))
    shared = {d: swap(parts[d]) for d in range(chips) if d != 1}
    if chips > 1:
        parts[1], shared = lax.optimization_barrier((parts[1], shared))
        shared[1] = swap(parts[1])
    return tuple(
        call(
            functools.partial(run_kernel, heads, chips),
            [(intervals, b, r)] * 2,
            [
                pltpu.VMEM((r, b), F32),
                pltpu.VMEM((intervals, b, r), F32),
                pltpu.VMEM((intervals, b, r), F32),
                pltpu.SemaphoreType.DMA((2, intervals)),
            ],
            out_spec=HBM,
        )(*parts, *[shared[d] for d in range(chips)], matrices, constants, next_matrix, next_constant)
    )


def solution(mesh):
    spec = P(("rx", "ry"), None, None)
    return jax.shard_map(
        on_device, mesh=mesh, in_specs=(spec, spec), out_specs=(spec, spec), check_vma=False
    )
```
